32 devices in a mesh: sky: 8 (over y, x, core), tm: 4 (over z).
Axes of the slice: x: 2, y: 2, z: 4, core: 2. Of those that a mesh axis runs over, the one named last changes fastest.
Arguments:
- residuals: float32 [262144], P(('sky', 'tm')), may hold values from -6 to 6
- weights: float32 [262144], P(('sky', 'tm')), may hold values from 0.1 to 10
- source_partials: bfloat16 [5, 262144], P(None, ('sky', 'tm')), may hold values from -1.5 to 1.5
- attitude_partials: bfloat16 [32, 262144], P(None, ('sky', 'tm')), may hold values from -0.025 to 0.045
- source_index: int32 [262144], P(('sky', 'tm')), may hold values from 0 to 4095, as said below
- tile_window: int32 [2048], P(('sky', 'tm')), may hold values from 0 to 511, as said below
- sources: float32 [5, 32768], P(None, 'sky'), may hold values from -6 to 6
- attitude: float32 [512, 32], P('tm'), may hold values from -6 to 6
- coupling: float32 [512], P('tm'), may hold values from 1 to 4
Outputs:
- new_sources: float32 [5, 32768], P(None, 'sky')
- new_attitude: float32 [512, 32], P('tm')
The draws below stay inside these ranges and needn't reach their ends.
Inputs may be any that keep to these rules, and one draw needn't show every extreme that they name: source_index counts among the 4096 sources of the sky region of the device that holds the observation (devices ordered sky first, then tm). The tiles held by the device at tm index t have tile_window from t * 128 to (t + 1) * 128 - 1.
All inputs are finite; a program needn't handle non-finite values.
Results may differ from the reference program's by a relative error of at most 0.00039.
Values sent between devices are 32-bit elements; how exact they have to be, the bound alone decides.
No kernel may reach another device: no remote copies, remote signals or barrier semaphores. Data moves between devices by JAX's collectives and lax.ppermute only.
A program may use at most 64 MiB of HBM per device.

```python
import math
import jax
import jax.numpy as jnp
from jax import lax

PARAMS = 5
KNOTS = 32
TILE = 128
ITERS = 8
OBS_DEV = 8192
S_DEV = 4096
W_DEV = 128
SOURCES = 32768
WINDOWS = 512
OBS = 262144
TILES_DEV = 64
TILES = 2048
N_TM = 4


def draw_source_index(key, part):
    return jax.random.randint(key, (OBS,), 0, S_DEV, dtype=jnp.int32)


def draw_tile_window(key, part):
    flat = jnp.arange(TILES, dtype=jnp.int32)
    device = flat // TILES_DEV
    time_block = device % N_TM
    offset = jax.random.randint(jax.random.fold_in(key, 7), (TILES,), 0, W_DEV, dtype=jnp.int32)
    return (time_block * W_DEV + offset).astype(jnp.int32)


def draw_attitude_partials(key, part):
    ranking = jax.random.permutation(jax.random.fold_in(key, 11), KNOTS)
    knot_signs = jnp.where(ranking < KNOTS // 2, 1.0, -1.0).astype(jnp.float32)
    common_key = jax.random.fold_in(key, 13)
    jitter_key = jax.random.fold_in(key, 17)
    shared_factor = jnp.clip(jax.random.normal(common_key, (OBS,), jnp.float32), -1.2, 1.2)
    jitter = jax.random.uniform(jitter_key, (KNOTS, OBS), jnp.float32, -0.01, 0.01)
    values = 0.01 + 0.02 * knot_signs[:, None] * shared_factor[None, :] + jitter
    return values.astype(jnp.bfloat16)


def steps_of(key, dims, pieces, least, largest):
    gain = 1.0
    for dim, shards_of in pieces:
        steps = jax.random.uniform(jax.random.fold_in(jax.random.fold_in(key, 6), dim), (shards_of,), jnp.float32, least / len(pieces), largest / len(pieces))
        gain = gain * jnp.repeat(jnp.exp(steps), dims[dim] // shards_of).reshape((-1,) + (1,) * (len(dims) - 1 - dim))
    return gain


def bell_draw(rng, dims, width, most, cuts=(), held_as=jnp.bfloat16):
    array = jax.random.normal(rng, dims, jnp.float32) * width
    if len(cuts) > 0:
        array = steps_of(rng, dims, cuts, -0.22, 0.18) * array
    return jnp.clip(array, min=-most, max=most).astype(held_as)


def setup_inputs(seed: int = 0) -> dict:
    seeds = jax.random.split(jax.random.key(seed), 10)
    residuals = bell_draw(seeds[0], (OBS,), 1.0, 6.0, ((0, 32),), jnp.float32)
    weights = jnp.clip(jnp.exp(math.log(10.0) - 4.6051702 * jax.random.uniform(seeds[1], (OBS,), jnp.float32) ** steps_of(seeds[1], (OBS,), ((0, 32),), -0.2, 0.2)), 0.1, 10.0)
    source_partials = bell_draw(seeds[2], (PARAMS, OBS), 0.25, 1.5, ((1, 32),))
    attitude_partials = draw_attitude_partials(jax.random.fold_in(seeds[9], 71), 0)
    source_index = draw_source_index(jax.random.fold_in(seeds[9], 71), 0)
    tile_window = draw_tile_window(jax.random.fold_in(seeds[9], 71), 0)
    sources = bell_draw(seeds[6], (PARAMS, SOURCES), 1.0, 6.0, ((1, 8),), jnp.float32)
    attitude = bell_draw(seeds[7], (WINDOWS, KNOTS), 1.0, 6.0, ((0, 4),), jnp.float32)
    coupling = jnp.clip(jnp.exp(math.log(4.0) - 1.3862944 * jax.random.uniform(seeds[8], (WINDOWS,), jnp.float32) ** steps_of(seeds[8], (WINDOWS,), ((0, 4),), -0.2, 0.2)), 1.0, 4.0)
    return {"residuals": residuals, "weights": weights, "source_partials": source_partials, "attitude_partials": attitude_partials, "source_index": source_index, "tile_window": tile_window, "sources": sources, "attitude": attitude, "coupling": coupling}


LOWER_PAIRS = tuple(((i, j) for i in range(5) for j in range(i + 1)))
DAMPING = 0.8
HIGHEST = lax.Precision.HIGHEST

def moment_rows(partials, weights, residuals):
    values = partials.astype(jnp.float32)
    entries = [weights * values[i] * values[j] for i, j in LOWER_PAIRS]
    entries = entries + [weights * values[i] * residuals for i in range(5)]
    return jnp.stack(entries)

def solve_sources(moments):
    matrix = {}
    for position, pair in enumerate(LOWER_PAIRS):
        matrix[pair] = moments[position] + (1.0 if pair[0] == pair[1] else 0.0)
    factor = {}
    for i in range(5):
        for j in range(i + 1):
            reduced = matrix[i, j]
            for k in range(j):
                reduced = reduced - factor[i, k] * factor[j, k]
            if i == j:
                factor[i, i] = jnp.sqrt(reduced)
            else:
                factor[i, j] = reduced / factor[j, j]
    forward = []
    for i in range(5):
        current = moments[15 + i]
        for k in range(i):
            current = current - factor[i, k] * forward[k]
        forward.append(current / factor[i, i])
    result = [None] * 5
    for i in reversed(range(5)):
        current = forward[i]
        for k in range(i + 1, 5):
            current = current - factor[k, i] * result[k]
        result[i] = current / factor[i, i]
    return jnp.stack(result)

def window_inverse(symmetric, left_coupling, right_coupling):
    knot_count = symmetric.shape[1]
    identity = jnp.eye(knot_count, dtype=jnp.float32)
    blocks = symmetric + (left_coupling + right_coupling)[:, None, None] * identity
    lower_factor = jnp.linalg.cholesky(blocks)
    inverse_factor = jax.scipy.linalg.solve_triangular(lower_factor, jnp.broadcast_to(identity, blocks.shape), lower=True)
    return jnp.einsum('wlk,wlm->wkm', inverse_factor, inverse_factor, precision=HIGHEST)

def apply_blocks(blocks, vectors):
    return jnp.einsum('wkl,wl->wk', blocks, vectors, precision=HIGHEST)

def global_index(source_index, block):
    start = (block * OBS_DEV).astype(jnp.int32)
    local = lax.dynamic_slice_in_dim(source_index, start, OBS_DEV, 0)
    offset = (block // N_TM * S_DEV).astype(jnp.int32)
    return (local + offset).astype(jnp.int32)

def reference(residuals, weights, source_partials, attitude_partials, source_index, tile_window, sources, attitude, coupling):
    block_total = residuals.shape[0] // OBS_DEV
    tiles_block = OBS_DEV // TILE
    window_total = attitude.shape[0]
    knot_count = attitude.shape[1]

    def source_step(block, moments):
        start = (block * OBS_DEV).astype(jnp.int32)
        part_res = lax.dynamic_slice_in_dim(residuals, start, OBS_DEV, 0)
        part_weight = lax.dynamic_slice_in_dim(weights, start, OBS_DEV, 0)
        part_src = lax.dynamic_slice_in_dim(source_partials, start, OBS_DEV, 1)
        part_index = global_index(source_index, block)
        return moments.at[:, part_index].add(moment_rows(part_src, part_weight, part_res))
    moments = lax.fori_loop(0, block_total, source_step, jnp.zeros((20, sources.shape[1]), jnp.float32))
    source_change = solve_sources(moments)
    new_sources = sources + source_change

    def window_step(block, carry):
        normal, right_side = carry
        start = (block * OBS_DEV).astype(jnp.int32)
        part_res = lax.dynamic_slice_in_dim(residuals, start, OBS_DEV, 0)
        part_weight = lax.dynamic_slice_in_dim(weights, start, OBS_DEV, 0)
        part_src = lax.dynamic_slice_in_dim(source_partials, start, OBS_DEV, 1)
        part_att = lax.dynamic_slice_in_dim(attitude_partials, start, OBS_DEV, 1)
        part_index = global_index(source_index, block)
        picked = source_change[:, part_index]
        corrected = part_res - lax.optimization_barrier(jnp.sum(part_src.astype(jnp.float32) * picked, axis=0))
        weighted = (part_weight * corrected).astype(jnp.bfloat16)
        scaled = (part_weight[None, :] * part_att.astype(jnp.float32)).astype(jnp.bfloat16)
        shaped_att = part_att.reshape(knot_count, tiles_block, TILE).astype(jnp.float32)
        shaped_scaled = scaled.reshape(knot_count, tiles_block, TILE).astype(jnp.float32)
        tile_normal = jnp.einsum('ktp,ltp->tkl', shaped_scaled, shaped_att, precision=HIGHEST).reshape(tiles_block, knot_count * knot_count)
        tile_rhs = jnp.einsum('ktp,tp->tk', shaped_att, weighted.reshape(tiles_block, TILE).astype(jnp.float32), precision=HIGHEST)
        tile_start = (block * tiles_block).astype(jnp.int32)
        windows = lax.dynamic_slice_in_dim(tile_window, tile_start, tiles_block, 0)
        return (normal.at[windows].add(tile_normal), right_side.at[windows].add(tile_rhs))
    start_carry = (jnp.zeros((window_total, knot_count * knot_count), jnp.float32), jnp.zeros((window_total, knot_count), jnp.float32))
    normal, right_side = lax.fori_loop(0, block_total, window_step, start_carry)
    normal = normal.reshape(window_total, knot_count, knot_count)
    symmetric = 0.5 * (normal + jnp.swapaxes(normal, 1, 2))
    zero_one = jnp.zeros((1,), jnp.float32)
    left_coupling = jnp.concatenate([zero_one, coupling[:-1]])
    right_coupling = jnp.concatenate([coupling[:-1], zero_one])
    inverse = window_inverse(symmetric, left_coupling, right_coupling)
    change = DAMPING * apply_blocks(inverse, right_side)
    for sweep in range(ITERS - 1):
        padded = jnp.pad(change, ((1, 1), (0, 0)))
        applied = apply_blocks(symmetric, change) + (left_coupling + right_coupling)[:, None] * change
        applied = applied - left_coupling[:, None] * padded[:-2] - right_coupling[:, None] * padded[2:]
        change = change + DAMPING * apply_blocks(inverse, right_side - applied)
    return (new_sources, attitude + change)
```

```python
import functools

import jax
import jax.numpy as jnp
from jax import lax
from jax.experimental import pallas as pl
from jax.experimental.pallas import tpu as pltpu
from jax.sharding import PartitionSpec as P

TILE = 128
ITERS = 8
DAMPING = 0.8
PARAMS = 5
PAIRS = tuple((i, j) for i in range(PARAMS) for j in range(i + 1))
MOMENTS = len(PAIRS) + PARAMS
LANES = 128
SPLITS = 3
CHUNK = 1024
ROWS = CHUNK // TILE
F32 = jnp.float32
BF16 = jnp.bfloat16
NT = (((1,), (1,)), ((), ()))
VMEM_LIMIT = 48 * 1024 * 1024


def vmem():
    return pl.BlockSpec(memory_space=pltpu.VMEM)


def smem():
    return pl.BlockSpec(memory_space=pltpu.SMEM)


def call(kernel, out_shape, in_specs, scratch=(), flops=0, traffic=0):
    return pl.pallas_call(
        kernel,
        out_shape=out_shape,
        in_specs=in_specs,
        out_specs=jax.tree.map(lambda _: vmem(), out_shape),
        scratch_shapes=list(scratch),
        compiler_params=pltpu.CompilerParams(vmem_limit_bytes=VMEM_LIMIT),
        cost_estimate=pl.CostEstimate(flops=flops, bytes_accessed=traffic, transcendentals=0),
    )


def iota(shape, dim):
    return lax.broadcasted_iota(jnp.int32, shape, dim)


def split_bf16(x, parts):
    out = []
    for part in range(parts):
        head = x.astype(BF16)
        out.append(head)
        if part < parts - 1:
            x = x - head.astype(F32)
    return out


def low_one_hot(row, half, low_count):
    low = (row // half) * LANES + (row & (LANES - 1))
    return jnp.where(iota((low_count, LANES), 0) == low, 1.0, 0.0).astype(BF16)


def high_digit(row, half):
    return (row & (half - 1)) // LANES


def moments_kernel(hi_count, me_ref, src_ref, w_ref, r_ref, sp_ref, tie_ref, *refs):
    peers = len(refs) - 4
    outs, (lhs, rhs, acc, blocks) = refs[:peers], refs[peers:]
    half = hi_count * LANES
    low_count = rhs.shape[0]
    acc[...] = jnp.zeros_like(acc)

    def chunk(c, carry):
        base = pl.multiple_of(c * ROWS, ROWS)
        src = src_ref[pl.ds(base, ROWS), :]
        w = w_ref[pl.ds(base, ROWS), :]
        r = r_ref[pl.ds(base, ROWS), :]
        columns = [
            sp_ref[:, pl.ds(pl.multiple_of((base + i) * TILE, TILE), TILE)].astype(F32)
            for i in range(ROWS)
        ]
        a = [
            jnp.concatenate([columns[i][p : p + 1] for i in range(ROWS)], axis=0)
            for p in range(PARAMS)
        ]
        wa = [w * x for x in a]
        sums = [wa[i] * a[j] for i, j in PAIRS] + [x * r for x in wa]
        parts = [[piece.astype(F32) for piece in split_bf16(s, SPLITS)] for s in sums]
        for i in range(ROWS):
            lanes = slice(i * TILE, (i + 1) * TILE)
            row = src[i : i + 1]
            rhs[:, lanes] = low_one_hot(row, half, low_count)
            mask = jnp.where(iota((hi_count, LANES), 0) == high_digit(row, half), 1.0, 0.0).astype(BF16)
            for s in range(SPLITS):
                for p in range(MOMENTS):
                    value = jnp.broadcast_to(parts[p][s][i : i + 1], (hi_count, LANES)).astype(BF16)
                    start = (s * MOMENTS + p) * hi_count
                    lhs[start : start + hi_count, lanes] = value * mask
        acc[...] += lax.dot_general(lhs[...], rhs[...], NT, preferred_element_type=F32)
        return carry

    lax.fori_loop(0, src_ref.shape[0] // ROWS, chunk, 0)
    rows = blocks.shape[2]
    for p in range(MOMENTS):
        total = acc[p * hi_count : (p + 1) * hi_count, :]
        for s in range(1, SPLITS):
            start = (s * MOMENTS + p) * hi_count
            total = total + acc[start : start + hi_count, :]
        for j in range(peers):
            q, first = divmod(j * rows, hi_count)
            blocks[j, p] = total[first : first + rows, q * LANES : (q + 1) * LANES]
    for j in range(peers):
        blocks[j, MOMENTS] = jnp.broadcast_to(tie_ref[...], (rows, LANES))
    me = me_ref[0]
    for k in range(peers):
        outs[k][...] = blocks[me ^ k]


def normals_kernel(win_ref, w_ref, att_ref, out_ref):
    windows = out_ref.shape[0]
    knots = att_ref.shape[0]
    copies = LANES // knots
    out_ref[...] = jnp.zeros_like(out_ref)
    blank = jnp.zeros((knots, TILE), BF16)
    lane = iota((8, LANES), 1)

    def pair(u, carry):
        att = att_ref[:, pl.ds(pl.multiple_of(u * 2 * TILE, 2 * TILE), 2 * TILE)]
        w = jnp.concatenate([w_ref[pl.ds(2 * u, 1), :], w_ref[pl.ds(2 * u + 1, 1), :]], axis=1)
        scaled = (w * att.astype(F32)).astype(BF16)
        left = jnp.concatenate([scaled[:, :TILE], blank], axis=1)
        right = jnp.concatenate([blank, scaled[:, TILE:]], axis=1)
        normal = lax.dot_general(
            jnp.concatenate([left, right], axis=0),
            jnp.concatenate([att] * copies, axis=0),
            NT,
            preferred_element_type=F32,
        )
        for h in range(2):
            value = normal[h * knots : h * knots + 8]
            for g in range(1, copies):
                start = h * knots + 8 * g
                value = jnp.where(lane < g * knots, value, normal[start : start + 8])
            slot = lax.rem(win_ref[2 * u + h], windows)
            out_ref[slot] += value
        return carry

    lax.fori_loop(0, w_ref.shape[0] // 2, pair, 0, unroll=4)


def solve_kernel(me_ref, *refs):
    peers = len(refs) - 3
    blocks, (change_ref, ties_ref, rows_scr) = refs[:peers], refs[peers:]
    moments = blocks[0][0:MOMENTS]
    for other in blocks[1:]:
        moments = moments + other[0:MOMENTS]
    matrix = {}
    for position, (i, j) in enumerate(PAIRS):
        matrix[i, j] = moments[position] + (1.0 if i == j else 0.0)
    factor, inverse = {}, {}
    for i in range(PARAMS):
        for j in range(i + 1):
            reduced = matrix[i, j]
            for k in range(j):
                reduced = reduced - factor[i, k] * factor[j, k]
            if i == j:
                factor[i, i] = jnp.sqrt(reduced)
                inverse[i] = 1.0 / factor[i, i]
            else:
                factor[i, j] = reduced * inverse[j]
    forward = []
    for i in range(PARAMS):
        current = moments[len(PAIRS) + i]
        for k in range(i):
            current = current - factor[i, k] * forward[k]
        forward.append(current * inverse[i])
    result = [None] * PARAMS
    for i in reversed(range(PARAMS)):
        current = forward[i]
        for k in range(i + 1, PARAMS):
            current = current - factor[k, i] * result[k]
        result[i] = current * inverse[i]
        change_ref[i] = result[i]
    me = me_ref[0]
    for k in range(peers):
        rows_scr[me ^ k] = jnp.broadcast_to(blocks[k][MOMENTS, 0:1, :], (8, LANES))
    first, last = me == 0, me == peers - 1
    own = rows_scr[me]
    before = jnp.where(first, 0.0, rows_scr[jnp.maximum(me - 1, 0)])
    after = jnp.where(last, 0.0, rows_scr[jnp.minimum(me + 1, peers - 1)])
    lane = iota((8, LANES), 1)
    own = jnp.where(jnp.logical_and(last, lane == LANES - 1), 0.0, own)
    own_left = jnp.where(lane == 0, pltpu.roll(before, 1, 1), pltpu.roll(own, 1, 1))
    low, high = lane < ITERS - 1, lane > LANES - ITERS
    rim_right = jnp.where(low, after, jnp.where(high, before, 0.0))
    after_left = jnp.where(lane == 0, pltpu.roll(own, 1, 1), pltpu.roll(after, 1, 1))
    rim_left = jnp.where(low, after_left, jnp.where(high, pltpu.roll(before, 1, 1), 0.0))
    ties_ref[0] = own_left
    ties_ref[1] = own
    ties_ref[2] = rim_left
    ties_ref[3] = rim_right


def invert_kernel(sky_ref, part_ref, ties_ref, out_ref, flat, cells):
    devices, own, eight, _ = part_ref.shape
    knots = cells.shape[0] // 32 if False else 32
    total = part_ref[0]
    for s in range(1, devices):
        total = total + part_ref[s]
    flat[...] = jnp.zeros_like(flat)
    flat[0 : own * 8, :] = total.reshape(own * 8, LANES)
    groups = LANES // knots
    for r in range(8):
        turned = flat[pl.ds(r, LANES, stride=8), :].T
        for g in range(groups):
            cells[(8 * g + r) * knots : (8 * g + r + 1) * knots, :] = turned[g * knots : (g + 1) * knots]
    shift = lax.rem(LANES - sky_ref[0] * own, LANES)
    ties = pltpu.roll(ties_ref[0] + ties_ref[1], shift, 1)
    diagonal = jnp.concatenate([ties] * (knots // 8), axis=0)
    inner = iota((knots, LANES), 0)
    blocks = []
    for k in range(knots):
        row = 0.5 * (cells[k * knots : (k + 1) * knots, :] + cells[pl.ds(k, knots, stride=knots), :])
        blocks.append(jnp.where(inner == k, row + diagonal, row))
    for k in range(knots):
        cells[k * knots : (k + 1) * knots, :] = blocks[k]

    def sweep(k, carry):
        at = pl.multiple_of(k * knots, knots)
        row = cells[pl.ds(at, knots), :]
        pivot = 1.0 / cells[pl.ds(at + k, 1), :]
        here = inner == k
        scaled = jnp.where(here, -pivot, row * pivot)
        for i in range(knots):
            old = jnp.where(here, 0.0, cells[i * knots : (i + 1) * knots, :])
            cells[i * knots : (i + 1) * knots, :] = old - row[i : i + 1] * scaled
        cells[pl.ds(at, knots), :] = scaled
        return carry

    lax.fori_loop(0, knots, sweep, 0)
    for r in range(8):
        turned = jnp.concatenate(
            [cells[(8 * g + r) * knots : (8 * g + r + 1) * knots, :] for g in range(groups)], axis=0
        ).T
        flat[pl.ds(r, LANES, stride=8), :] = -turned
    out_ref[...] = flat[0 : own * 8, :].reshape(own, 8, LANES)


def rhs_kernel(hi_count, me_ref, win_ref, src_ref, w_ref, r_ref, sp_ref, att_ref, sources_ref, inv_ref, *refs):
    peers = len(refs) - 7
    blocks = refs[:peers]
    new_ref, out_ref, changes, table, rhs, chosen, weighted = refs[peers:]
    half = hi_count * LANES
    low_count = rhs.shape[0]
    windows = LANES
    knots = att_ref.shape[0]
    own = inv_ref.shape[0]
    me = me_ref[0]
    for k in range(peers):
        changes[me ^ k] = blocks[k][...]
    rows = blocks[0].shape[1]
    for j in range(peers):
        q, first = divmod(j * rows, hi_count)
        for p in range(PARAMS):
            value = changes[j, p]
            for s, piece in enumerate(split_bf16(value, SPLITS)):
                start = (s * PARAMS + p) * hi_count + first
                table[start : start + rows, q * LANES : (q + 1) * LANES] = piece.astype(F32)
        for i in range(rows):
            lanes = slice((j * rows + i) * LANES, (j * rows + i + 1) * LANES)
            step = jnp.concatenate([changes[j, p, i : i + 1, :] for p in range(PARAMS)], axis=0)
            new_ref[:, lanes] = sources_ref[:, lanes] + step
    lookup = table[...].astype(BF16)

    def chunk(c, total):
        base = pl.multiple_of(c * ROWS, ROWS)
        src = src_ref[pl.ds(base, ROWS), :]
        w = w_ref[pl.ds(base, ROWS), :]
        r = r_ref[pl.ds(base, ROWS), :]
        for i in range(ROWS):
            rhs[:, i * TILE : (i + 1) * TILE] = low_one_hot(src[i : i + 1], half, low_count)
        chosen[...] = jnp.dot(lookup, rhs[...], preferred_element_type=F32)
        for i in range(ROWS):
            lanes = slice(i * TILE, (i + 1) * TILE)
            columns = sp_ref[:, pl.ds(pl.multiple_of((base + i) * TILE, TILE), TILE)].astype(F32)
            model = jnp.zeros((hi_count, LANES), F32)
            for p in range(PARAMS):
                value = chosen[p * hi_count : (p + 1) * hi_count, lanes]
                for s in range(1, SPLITS):
                    start = (s * PARAMS + p) * hi_count
                    value = value + chosen[start : start + hi_count, lanes]
                model = model + value * columns[p : p + 1]
            here = iota((hi_count, LANES), 0) == high_digit(src[i : i + 1], half)
            model = jnp.sum(jnp.where(here, model, 0.0), axis=0, keepdims=True)
            change = w[i : i + 1] * (r[i : i + 1] - model)
            slot = lax.rem(win_ref[base + i], windows)
            weighted[:, lanes] = jnp.where(iota((windows, LANES), 0) == slot, change, 0.0).astype(BF16)
        att = att_ref[:, pl.ds(pl.multiple_of(base * TILE, CHUNK), CHUNK)]
        return total + lax.dot_general(att, weighted[...], NT, preferred_element_type=F32)

    total = lax.fori_loop(0, src_ref.shape[0] // ROWS, chunk, jnp.zeros((knots, windows), F32))
    out_ref[0:own] = inv_ref[...]
    out_ref[own : own + knots // 8] = total.reshape(knots // 8, 8, LANES)


def rim_kernel(all_ref, low_ref, high_ref, main_ref):
    devices, blocks, _, _ = all_ref.shape
    own = blocks - 4
    sides = all_ref[0, own:blocks]
    for s in range(1, devices):
        sides = sides + all_ref[s, own:blocks]
    main_ref[...] = sides
    low_ref[8:12] = sides
    high_ref[8:12] = sides
    for w in range(8):
        low_ref[w] = all_ref[w // own, w % own]
        far = devices * own - 8 + w
        high_ref[w] = all_ref[far // own, far % own]


def turn_kernel(all_ref, main_ref, flat):
    devices, blocks, _, _ = all_ref.shape
    own = blocks - 4
    knots = 32
    groups = LANES // knots
    for s in range(devices):
        flat[s * own * 8 : (s + 1) * own * 8, :] = all_ref[s, 0:own].reshape(own * 8, LANES)
    for r in range(8):
        turned = flat[pl.ds(r, LANES, stride=8), :].T
        for g in range(groups):
            main_ref[(8 * g + r) * knots : (8 * g + r + 1) * knots, :] = turned[g * knots : (g + 1) * knots]


def sweeps_kernel(main_ref, sides_ref, low_ref, high_ref, ties_ref, attitude_ref, out_ref, flat, rim, vector):
    knots = attitude_ref.shape[1]
    groups = LANES // knots
    flat[...] = jnp.zeros_like(flat)
    flat[0:64, :] = low_ref[0:8].reshape(64, LANES)
    flat[960:1024, :] = high_ref[0:8].reshape(64, LANES)
    for r in range(8):
        turned = flat[pl.ds(r, LANES, stride=8), :].T
        for g in range(groups):
            rim[(8 * g + r) * knots : (8 * g + r + 1) * knots, :] = turned[g * knots : (g + 1) * knots]
    lane = iota((knots, LANES), 1)
    rim_sides = jnp.where(
        lane < ITERS - 1,
        low_ref[8:12].reshape(knots, LANES),
        jnp.where(lane > LANES - ITERS, high_ref[8:12].reshape(knots, LANES), 0.0),
    )
    sides = jnp.concatenate([sides_ref[...].reshape(knots, LANES), rim_sides], axis=1)

    def wide(a, b):
        return DAMPING * jnp.concatenate([jnp.concatenate([a, b], axis=1)] * (knots // 8), axis=0)

    left = wide(ties_ref[0], ties_ref[2])
    right = wide(ties_ref[1], ties_ref[3])

    def applied(x):
        vector[...] = x
        main = jnp.zeros((knots, LANES), F32)
        side = jnp.zeros((knots, LANES), F32)
        for k in range(knots):
            row = vector[k : k + 1, :]
            main = main + main_ref[k * knots : (k + 1) * knots, :] * row[:, :LANES]
            side = side + rim[k * knots : (k + 1) * knots, :] * row[:, LANES:]
        return jnp.concatenate([main, side], axis=1)

    first = applied(DAMPING * sides)

    def sweep(_, change):
        ends = left * pltpu.roll(change, 1, 1) + right * pltpu.roll(change, 2 * LANES - 1, 1)
        return (1.0 - DAMPING) * change + first + applied(ends)

    change = lax.fori_loop(0, ITERS - 1, sweep, first)
    out_ref[...] = attitude_ref[...] + change[:, :LANES].T


def on_device(
    residuals, weights, source_partials, attitude_partials, source_index, tile_window, sources, attitude, coupling
):
    peers = lax.axis_size("tm")
    devices = lax.axis_size("sky")
    source_count = sources.shape[1]
    windows, knots = attitude.shape
    tiles = residuals.shape[0] // TILE
    own = windows // devices
    rows = source_count // LANES // peers
    hi_count = source_count // (2 * LANES)
    low_count = 2 * LANES
    me = lax.axis_index("tm").astype(jnp.int32).reshape(1)
    sky = lax.axis_index("sky").astype(jnp.int32).reshape(1)
    src = source_index.reshape(tiles, TILE)
    w = weights.reshape(tiles, TILE)
    r = residuals.reshape(tiles, TILE)

    def exchanged(blocks):
        return [blocks[0]] + [
            lax.ppermute(blocks[k], "tm", [(i, i ^ k) for i in range(peers)]) for k in range(1, peers)
        ]

    block = jax.ShapeDtypeStruct((MOMENTS + 1, rows, LANES), F32)
    with jax.named_scope("moments"):
        blocks = call(
            functools.partial(moments_kernel, hi_count),
            [block] * peers,
            [smem()] + [vmem()] * 5,
            [
                pltpu.VMEM((SPLITS * MOMENTS * hi_count, CHUNK), BF16),
                pltpu.VMEM((low_count, CHUNK), BF16),
                pltpu.VMEM((SPLITS * MOMENTS * hi_count, low_count), F32),
                pltpu.VMEM((peers, MOMENTS + 1, rows, LANES), F32),
            ],
        )(me, src, w, r, source_partials, coupling.reshape(1, windows))
    blocks = exchanged(blocks)
    with jax.named_scope("normals"):
        normals = call(
            normals_kernel,
            jax.ShapeDtypeStruct((windows, knots * knots // LANES, LANES), F32),
            [smem(), vmem(), vmem()],
        )(tile_window, w, attitude_partials)
    parts = lax.all_to_all(
        normals.reshape(devices, own, knots * knots // LANES, LANES), "sky", 0, 0, tiled=True
    )
    with jax.named_scope("solve"):
        change, ties = call(
            solve_kernel,
            [
                jax.ShapeDtypeStruct((PARAMS, rows, LANES), F32),
                jax.ShapeDtypeStruct((4, 8, LANES), F32),
            ],
            [smem()] + [vmem()] * peers,
            [pltpu.VMEM((peers, 8, LANES), F32)],
        )(me, *blocks)
    changes = exchanged([change] * peers)
    with jax.named_scope("invert"):
        inverse = call(
            invert_kernel,
            jax.ShapeDtypeStruct((own, knots * knots // LANES, LANES), F32),
            [smem(), vmem(), vmem()],
            [pltpu.VMEM((8 * LANES, LANES), F32), pltpu.VMEM((knots * knots, LANES), F32)],
        )(sky, parts, ties)
    with jax.named_scope("right_sides"):
        new_sources, part = call(
            functools.partial(rhs_kernel, hi_count),
            [
                jax.ShapeDtypeStruct(sources.shape, F32),
                jax.ShapeDtypeStruct((own + knots // 8, 8, LANES), F32),
            ],
            [smem(), smem()] + [vmem()] * (7 + peers),
            [
                pltpu.VMEM((peers, PARAMS, rows, LANES), F32),
                pltpu.VMEM((SPLITS * PARAMS * hi_count, low_count), F32),
                pltpu.VMEM((low_count, CHUNK), BF16),
                pltpu.VMEM((SPLITS * PARAMS * hi_count, CHUNK), F32),
                pltpu.VMEM((windows, CHUNK), BF16),
            ],
        )(me, tile_window, src, w, r, source_partials, attitude_partials, sources, inverse, *changes)
    gathered = lax.all_gather(part, "sky", axis=0, tiled=False)
    with jax.named_scope("rims"):
        rim = jax.ShapeDtypeStruct((12, 8, LANES), F32)
        low, high, sides = call(
            rim_kernel, [rim, rim, jax.ShapeDtypeStruct((4, 8, LANES), F32)], [vmem()]
        )(gathered)
    after = lax.ppermute(low, "tm", [(i, i - 1) for i in range(1, peers)])
    before = lax.ppermute(high, "tm", [(i, i + 1) for i in range(peers - 1)])
    with jax.named_scope("turn"):
        main = call(
            turn_kernel,
            jax.ShapeDtypeStruct((knots * knots, LANES), F32),
            [vmem()],
            [pltpu.VMEM((8 * LANES, LANES), F32)],
        )(gathered)
    with jax.named_scope("sweeps"):
        new_attitude = call(
            sweeps_kernel,
            jax.ShapeDtypeStruct(attitude.shape, F32),
            [vmem()] * 6,
            [
                pltpu.VMEM((8 * LANES, LANES), F32),
                pltpu.VMEM((knots * knots, LANES), F32),
                pltpu.VMEM((knots, 2 * LANES), F32),
            ],
        )(main, sides, after, before, ties, attitude)
    return new_sources, new_attitude


def solution(mesh):
    return jax.shard_map(
        on_device,
        mesh=mesh,
        in_specs=(
            P(("sky", "tm")),
            P(("sky", "tm")),
            P(None, ("sky", "tm")),
            P(None, ("sky", "tm")),
            P(("sky", "tm")),
            P(("sky", "tm")),
            P(None, "sky"),
            P("tm", None),
            P("tm"),
        ),
        out_specs=(P(None, "sky"), P("tm", None)),
        check_vma=False,
    )
```

```python
import functools
import math

import jax
import jax.numpy as jnp
from jax import lax
from jax.experimental import pallas as pl
from jax.experimental.pallas import tpu as pltpu
from jax.sharding import PartitionSpec as P

TILE = 128
ITERS = 8
RIM = ITERS - 1
DAMPING = 0.8
PARAMS = 5
PAIRS = tuple((i, j) for i in range(PARAMS) for j in range(i + 1))
MOMENTS = len(PAIRS) + PARAMS
LANES = 128
CORES = 2
HALF = LANES // CORES
SPLITS = 3
CHUNK = 1024
ROWS = CHUNK // TILE
F32 = jnp.float32
BF16 = jnp.bfloat16
NT = (((1,), (1,)), ((), ()))
FLOPS_MICRO = 1e9
VMEM_LIMIT = 48 * 1024 * 1024


def vmem():
    return pl.BlockSpec(memory_space=pltpu.VMEM)


def smem():
    return pl.BlockSpec(memory_space=pltpu.SMEM)


def call(kernel, out_shape, in_specs, scratch=(), micros=0.1, limit=VMEM_LIMIT):
    return pl.pallas_call(
        kernel,
        out_shape=out_shape,
        in_specs=in_specs,
        out_specs=jax.tree.map(lambda _: vmem(), out_shape),
        scratch_shapes=list(scratch),
        compiler_params=pltpu.CompilerParams(vmem_limit_bytes=limit),
        cost_estimate=pl.CostEstimate(flops=int(micros * FLOPS_MICRO), bytes_accessed=0, transcendentals=0),
    )


def iota(shape, dim):
    return lax.broadcasted_iota(jnp.int32, shape, dim)


def split_bf16(x, parts):
    out = []
    for part in range(parts):
        head = x.astype(BF16)
        out.append(head)
        if part < parts - 1:
            x = x - head.astype(F32)
    return out


def low_one_hot(row, half, low_count):
    low = (row // half) * LANES + (row & (LANES - 1))
    return jnp.where(iota((low_count, LANES), 0) == low, 1.0, 0.0).astype(BF16)


def high_digit(row, half):
    return (row & (half - 1)) // LANES


def moments_kernel(hi_count, me_ref, src_hbm, w_hbm, r_hbm, sp_hbm, tie_hbm, *refs):
    peers = len(refs) - 10
    outs, (lhs, rhs, acc, blocks, src_ref, w_ref, r_ref, sp_ref, tie_ref, sems) = refs[:peers], refs[peers:]
    pairs = ((src_hbm, src_ref), (w_hbm, w_ref), (r_hbm, r_ref), (sp_hbm, sp_ref), (tie_hbm, tie_ref))
    copies = [pltpu.make_async_copy(a, b, sems.at[i]) for i, (a, b) in enumerate(pairs)]
    for copy in copies:
        copy.start()
    half = hi_count * LANES
    low_count = rhs.shape[0]
    acc[...] = jnp.zeros_like(acc)
    for copy in copies:
        copy.wait()

    def chunk(c, carry):
        base = pl.multiple_of(c * ROWS, ROWS)
        src = src_ref[pl.ds(base, ROWS), :]
        w = w_ref[pl.ds(base, ROWS), :]
        r = r_ref[pl.ds(base, ROWS), :]
        columns = [
            sp_ref[:, pl.ds(pl.multiple_of((base + i) * TILE, TILE), TILE)].astype(F32)
            for i in range(ROWS)
        ]
        a = [
            jnp.concatenate([columns[i][p : p + 1] for i in range(ROWS)], axis=0)
            for p in range(PARAMS)
        ]
        wa = [w * x for x in a]
        sums = [wa[i] * a[j] for i, j in PAIRS] + [x * r for x in wa]
        parts = [[piece.astype(F32) for piece in split_bf16(s, SPLITS)] for s in sums]
        for i in range(ROWS):
            lanes = slice(i * TILE, (i + 1) * TILE)
            row = src[i : i + 1]
            rhs[:, lanes] = low_one_hot(row, half, low_count)
            mask = jnp.where(iota((hi_count, LANES), 0) == high_digit(row, half), 1.0, 0.0).astype(BF16)
            for s in range(SPLITS):
                for p in range(MOMENTS):
                    value = jnp.broadcast_to(parts[p][s][i : i + 1], (hi_count, LANES)).astype(BF16)
                    start = (s * MOMENTS + p) * hi_count
                    lhs[start : start + hi_count, lanes] = value * mask
        acc[...] += lax.dot_general(lhs[...], rhs[...], NT, preferred_element_type=F32)
        return carry

    lax.fori_loop(0, src_ref.shape[0] // ROWS, chunk, 0)
    rows = blocks.shape[2]
    for p in range(MOMENTS):
        total = acc[p * hi_count : (p + 1) * hi_count, :]
        for s in range(1, SPLITS):
            start = (s * MOMENTS + p) * hi_count
            total = total + acc[start : start + hi_count, :]
        for j in range(peers):
            q, first = divmod(j * rows, hi_count)
            blocks[j, p] = total[first : first + rows, q * LANES : (q + 1) * LANES]
    for j in range(peers):
        blocks[j, MOMENTS] = jnp.broadcast_to(tie_ref[...], (rows, LANES))
    me = me_ref[0]
    for k in range(peers):
        outs[k][...] = blocks[me ^ k]


def normals_kernel(chips, win_ref, w_ref, att_ref, out_ref):
    windows = out_ref.shape[0]
    own = windows // chips // CORES
    knots = att_ref.shape[0]
    copies = LANES // knots
    out_ref[...] = jnp.zeros_like(out_ref)
    blank = jnp.zeros((knots, TILE), BF16)
    lane = iota((8, LANES), 1)

    def pair(u, carry):
        att = att_ref[:, pl.ds(pl.multiple_of(u * 2 * TILE, 2 * TILE), 2 * TILE)]
        w = jnp.concatenate([w_ref[pl.ds(2 * u, 1), :], w_ref[pl.ds(2 * u + 1, 1), :]], axis=1)
        scaled = (w * att.astype(F32)).astype(BF16)
        left = jnp.concatenate([scaled[:, :TILE], blank], axis=1)
        right = jnp.concatenate([blank, scaled[:, TILE:]], axis=1)
        normal = lax.dot_general(
            jnp.concatenate([left, right], axis=0),
            jnp.concatenate([att] * copies, axis=0),
            NT,
            preferred_element_type=F32,
        )
        for h in range(2):
            value = normal[h * knots : h * knots + 8]
            for g in range(1, copies):
                start = h * knots + 8 * g
                value = jnp.where(lane < g * knots, value, normal[start : start + 8])
            slot = lax.rem(win_ref[2 * u + h], windows)
            block = slot // own
            device = lax.rem(block, chips) * CORES + block // chips
            out_ref[device * own + lax.rem(slot, own)] += value
        return carry

    lax.fori_loop(0, w_ref.shape[0] // 2, pair, 0, unroll=4)


def solve_kernel(me_ref, sky_ref, *refs):
    peers = len(refs) - 3
    blocks, (change_ref, ties_ref, rows_scr) = refs[:peers], refs[peers:]
    moments = blocks[0][0:MOMENTS]
    for other in blocks[1:]:
        moments = moments + other[0:MOMENTS]
    matrix = {}
    for position, (i, j) in enumerate(PAIRS):
        matrix[i, j] = moments[position] + (1.0 if i == j else 0.0)
    factor, inverse = {}, {}
    for i in range(PARAMS):
        for j in range(i + 1):
            reduced = matrix[i, j]
            for k in range(j):
                reduced = reduced - factor[i, k] * factor[j, k]
            if i == j:
                factor[i, i] = jnp.sqrt(reduced)
                inverse[i] = 1.0 / factor[i, i]
            else:
                factor[i, j] = reduced * inverse[j]
    forward = []
    for i in range(PARAMS):
        current = moments[len(PAIRS) + i]
        for k in range(i):
            current = current - factor[i, k] * forward[k]
        forward.append(current * inverse[i])
    result = [None] * PARAMS
    for i in reversed(range(PARAMS)):
        current = forward[i]
        for k in range(i + 1, PARAMS):
            current = current - factor[k, i] * result[k]
        result[i] = current * inverse[i]
        change_ref[i] = result[i]
    me, core = me_ref[0], lax.rem(sky_ref[0], CORES)
    for k in range(peers):
        rows_scr[me ^ k] = jnp.broadcast_to(blocks[k][MOMENTS, 0:1, :], (8, LANES))
    first, last = me == 0, me == peers - 1
    own = rows_scr[me]
    before = jnp.where(first, 0.0, rows_scr[jnp.maximum(me - 1, 0)])
    after = jnp.where(last, 0.0, rows_scr[jnp.minimum(me + 1, peers - 1)])
    lane = iota((8, LANES), 1)
    own = jnp.where(jnp.logical_and(last, lane == LANES - 1), 0.0, own)
    own_left = jnp.where(lane == 0, pltpu.roll(before, 1, 1), pltpu.roll(own, 1, 1))
    after_left = jnp.where(lane == 0, pltpu.roll(own, 1, 1), pltpu.roll(after, 1, 1))
    before_left = pltpu.roll(before, 1, 1)
    ties_ref[0] = own_left + own

    def placed(before, own, after):
        low = jnp.where(lane < HALF + RIM, own, jnp.where(lane >= LANES - RIM, before, 0.0))
        high = jnp.where(lane < RIM, after, jnp.where(lane >= HALF - RIM, own, 0.0))
        return jnp.where(core == 0, low, pltpu.roll(high, HALF, 1))

    ties_ref[1] = placed(before_left, own_left, after_left)
    ties_ref[2] = placed(before, own, after)


def invert_kernel(sky_ref, part_ref, ties_ref, out_ref, flat, cells):
    devices, own, _, _ = part_ref.shape
    knots = math.isqrt(out_ref.shape[1] * LANES)
    total = part_ref[0]
    for s in range(1, devices):
        total = total + part_ref[s]
    flat[...] = jnp.zeros_like(flat)
    flat[0 : own * 8, :] = total.reshape(own * 8, LANES)
    groups = LANES // knots
    for r in range(8):
        turned = flat[pl.ds(r, LANES, stride=8), :].T
        for g in range(groups):
            cells[(8 * g + r) * knots : (8 * g + r + 1) * knots, :] = turned[g * knots : (g + 1) * knots]
    core, chip = lax.rem(sky_ref[0], CORES), sky_ref[0] // CORES
    shift = lax.rem(LANES - core * HALF - chip * own, LANES)
    ties = pltpu.roll(ties_ref[0], shift, 1)
    diagonal = jnp.concatenate([ties] * (knots // 8), axis=0)
    inner = iota((knots, LANES), 0)
    blocks = []
    for k in range(knots):
        row = 0.5 * (cells[k * knots : (k + 1) * knots, :] + cells[pl.ds(k, knots, stride=knots), :])
        blocks.append(jnp.where(inner == k, row + diagonal, row))
    for k in range(knots):
        cells[k * knots : (k + 1) * knots, :] = blocks[k]

    def sweep(k, carry):
        at = pl.multiple_of(k * knots, knots)
        row = cells[pl.ds(at, knots), :]
        pivot = 1.0 / cells[pl.ds(at + k, 1), :]
        here = inner == k
        scaled = jnp.where(here, -pivot, row * pivot)
        for i in range(knots):
            old = jnp.where(here, 0.0, cells[i * knots : (i + 1) * knots, :])
            cells[i * knots : (i + 1) * knots, :] = old - row[i : i + 1] * scaled
        cells[pl.ds(at, knots), :] = scaled
        return carry

    lax.fori_loop(0, knots, sweep, 0)
    for r in range(8):
        turned = jnp.concatenate(
            [cells[(8 * g + r) * knots : (8 * g + r + 1) * knots, :] for g in range(groups)], axis=0
        ).T
        flat[pl.ds(r, LANES, stride=8), :] = -turned
    out_ref[...] = flat[0 : own * 8, :].reshape(own, 8, LANES)


def rhs_kernel(hi_count, me_ref, win_ref, src_ref, w_ref, r_ref, sp_ref, att_ref, sources_ref, *refs):
    peers = len(refs) - 7
    blocks = refs[:peers]
    new_ref, out_ref, changes, table, rhs, chosen, weighted = refs[peers:]
    half = hi_count * LANES
    low_count = rhs.shape[0]
    windows = LANES
    knots = att_ref.shape[0]
    me = me_ref[0]
    for k in range(peers):
        changes[me ^ k] = blocks[k][...]
    rows = blocks[0].shape[1]
    for j in range(peers):
        q, first = divmod(j * rows, hi_count)
        for p in range(PARAMS):
            value = changes[j, p]
            for s, piece in enumerate(split_bf16(value, SPLITS)):
                start = (s * PARAMS + p) * hi_count + first
                table[start : start + rows, q * LANES : (q + 1) * LANES] = piece.astype(F32)
        for i in range(rows):
            lanes = slice((j * rows + i) * LANES, (j * rows + i + 1) * LANES)
            step = jnp.concatenate([changes[j, p, i : i + 1, :] for p in range(PARAMS)], axis=0)
            new_ref[:, lanes] = sources_ref[:, lanes] + step
    lookup = table[...].astype(BF16)

    def chunk(c, total):
        base = pl.multiple_of(c * ROWS, ROWS)
        src = src_ref[pl.ds(base, ROWS), :]
        w = w_ref[pl.ds(base, ROWS), :]
        r = r_ref[pl.ds(base, ROWS), :]
        for i in range(ROWS):
            rhs[:, i * TILE : (i + 1) * TILE] = low_one_hot(src[i : i + 1], half, low_count)
        chosen[...] = jnp.dot(lookup, rhs[...], preferred_element_type=F32)
        for i in range(ROWS):
            lanes = slice(i * TILE, (i + 1) * TILE)
            columns = sp_ref[:, pl.ds(pl.multiple_of((base + i) * TILE, TILE), TILE)].astype(F32)
            model = jnp.zeros((hi_count, LANES), F32)
            for p in range(PARAMS):
                value = chosen[p * hi_count : (p + 1) * hi_count, lanes]
                for s in range(1, SPLITS):
                    start = (s * PARAMS + p) * hi_count
                    value = value + chosen[start : start + hi_count, lanes]
                model = model + value * columns[p : p + 1]
            here = iota((hi_count, LANES), 0) == high_digit(src[i : i + 1], half)
            model = jnp.sum(jnp.where(here, model, 0.0), axis=0, keepdims=True)
            change = w[i : i + 1] * (r[i : i + 1] - model)
            slot = lax.rem(win_ref[base + i], windows)
            weighted[:, lanes] = jnp.where(iota((windows, LANES), 0) == slot, change, 0.0).astype(BF16)
        att = att_ref[:, pl.ds(pl.multiple_of(base * TILE, CHUNK), CHUNK)]
        return total + lax.dot_general(att, weighted[...], NT, preferred_element_type=F32)

    total = lax.fori_loop(0, src_ref.shape[0] // ROWS, chunk, jnp.zeros((knots, windows), F32))
    out_ref[...] = total


def send_kernel(sky_ref, inv_ref, mine_ref, theirs_ref, out_ref):
    own = inv_ref.shape[0]
    core = lax.rem(sky_ref[0], CORES)
    total = mine_ref[...] + theirs_ref[...]
    total = jnp.where(core == 0, total, pltpu.roll(total, HALF, 1))
    packed = narrow(total)
    out_ref[0:own] = inv_ref[...]
    out_ref[own:] = packed.reshape(packed.shape[0] // 8, 8, LANES)


def narrow(x):
    rows = x.shape[0] // 2
    low = iota((rows, LANES), 1) < HALF
    return jnp.where(low, x[:rows], pltpu.roll(x[rows:], HALF, 1))


def widen(x):
    return jnp.concatenate([x, pltpu.roll(x, HALF, 1)], axis=0)


def rim_kernel(sky_ref, *refs):
    chips = len(refs) - 3
    parts, (inner_ref, outer_ref, main_ref) = refs[:chips], refs[chips:]
    own = parts[0].shape[0] - (main_ref.shape[0] - HALF)
    core, chip = lax.rem(sky_ref[0], CORES), sky_ref[0] // CORES
    sides = parts[0][own:]
    for part in parts[1:]:
        sides = sides + part[own:]
    for k in range(chips):
        main_ref[pl.ds((chip ^ k) * own, own)] = parts[k][0:own]
    main_ref[HALF:] = sides
    inner_ref[0:8] = main_ref[pl.ds((1 - core) * (HALF - 8), 8)]
    outer_ref[0:8] = main_ref[pl.ds(core * (HALF - 8), 8)]
    inner_ref[8:] = sides
    outer_ref[8:] = sides


def sweeps_kernel(sky_ref, main_ref, inner_ref, outer_ref, ties_ref, out_ref, flat, cells, vector):
    knots = out_ref.shape[0]
    groups = LANES // knots
    core = lax.rem(sky_ref[0], CORES)
    low = jnp.where(core == 0, outer_ref[...], inner_ref[...])
    high = jnp.where(core == 0, inner_ref[...], outer_ref[...])
    flat[...] = jnp.zeros_like(flat)
    flat[0 : HALF * 8, :] = main_ref[0:HALF].reshape(HALF * 8, LANES)
    flat[HALF * 8 : HALF * 8 + 64, :] = high[0:8].reshape(64, LANES)
    flat[LANES * 8 - 64 : LANES * 8, :] = low[0:8].reshape(64, LANES)
    for r in range(8):
        turned = flat[pl.ds(r, LANES, stride=8), :].T
        for g in range(groups):
            cells[(8 * g + r) * knots : (8 * g + r + 1) * knots, :] = turned[g * knots : (g + 1) * knots]

    def wide(x):
        return widen(x.reshape(knots // 2, LANES))

    lane = iota((knots, LANES), 1)
    sides = jnp.where(lane < HALF, wide(main_ref[HALF:]), 0.0)
    sides = jnp.where(jnp.logical_and(lane >= HALF, lane < HALF + RIM), pltpu.roll(wide(high[8:]), HALF, 1), sides)
    sides = jnp.where(lane >= LANES - RIM, pltpu.roll(wide(low[8:]), HALF, 1), sides)
    left = DAMPING * jnp.concatenate([ties_ref[1]] * (knots // 8), axis=0)
    right = DAMPING * jnp.concatenate([ties_ref[2]] * (knots // 8), axis=0)

    def applied(x):
        vector[...] = x
        total = [jnp.zeros((knots, LANES), F32) for _ in range(4)]
        for k in range(knots):
            total[k % 4] += cells[k * knots : (k + 1) * knots, :] * vector[k : k + 1, :]
        return (total[0] + total[1]) + (total[2] + total[3])

    first = applied(DAMPING * sides)

    def sweep(_, change):
        ends = left * pltpu.roll(change, 1, 1) + right * pltpu.roll(change, LANES - 1, 1)
        return (1.0 - DAMPING) * change + first + applied(ends)

    out_ref[...] = lax.fori_loop(0, ITERS - 1, sweep, first)


def finish_kernel(sky_ref, mine_ref, theirs_ref, attitude_ref, out_ref):
    core = lax.rem(sky_ref[0], CORES)
    lower = jnp.where(core == 0, mine_ref[...], theirs_ref[...])
    upper = jnp.where(core == 0, theirs_ref[...], mine_ref[...])
    lane = iota(lower.shape, 1)
    out_ref[...] = attitude_ref[...] + jnp.where(lane < HALF, lower, pltpu.roll(upper, HALF, 1))


def on_device(
    residuals, weights, source_partials, attitude_partials, source_index, tile_window, sources, attitude, coupling
):
    peers = lax.axis_size("tm")
    devices = lax.axis_size("sky")
    source_count = sources.shape[1]
    windows, knots = attitude.shape
    tiles = residuals.shape[0] // TILE
    own = windows // devices
    rows = source_count // LANES // peers
    hi_count = source_count // (2 * LANES)
    low_count = 2 * LANES
    me = lax.axis_index("tm").astype(jnp.int32).reshape(1)
    sky = lax.axis_index("sky").astype(jnp.int32).reshape(1)
    src = source_index.reshape(tiles, TILE)
    w = weights.reshape(tiles, TILE)
    r = residuals.reshape(tiles, TILE)

    chips = devices // CORES
    cell_rows = knots * knots // LANES

    def swapped(blocks):
        out = [blocks[0]] + [None] * (peers - 1)
        for k in sorted(range(1, peers), key=lambda k: (k < peers // 2, k)):
            out[k] = lax.ppermute(blocks[k], "tm", [(i, i ^ k) for i in range(peers)])
        return out

    def other_core(x):
        return lax.ppermute(x, "sky", [(i, i ^ 1) for i in range(devices)])

    block = jax.ShapeDtypeStruct((MOMENTS + 1, rows, LANES), F32)
    with jax.named_scope("moments"):
        blocks = call(
            functools.partial(moments_kernel, hi_count),
            [block] * peers,
            [smem()] + [pl.BlockSpec(memory_space=pl.ANY)] * 5,
            [
                pltpu.VMEM((SPLITS * MOMENTS * hi_count, CHUNK), BF16),
                pltpu.VMEM((low_count, CHUNK), BF16),
                pltpu.VMEM((SPLITS * MOMENTS * hi_count, low_count), F32),
                pltpu.VMEM((peers, MOMENTS + 1, rows, LANES), F32),
                pltpu.VMEM(src.shape, jnp.int32),
                pltpu.VMEM(w.shape, F32),
                pltpu.VMEM(r.shape, F32),
                pltpu.VMEM(source_partials.shape, BF16),
                pltpu.VMEM((1, windows), F32),
                pltpu.SemaphoreType.DMA((5,)),
            ],
            micros=7.5,
            limit=60 * 1024 * 1024,
        )(me, src, w, r, source_partials, coupling.reshape(1, windows))
    blocks, tile_window = lax.optimization_barrier((blocks, tile_window))
    blocks = swapped(blocks)
    with jax.named_scope("normals"):
        normals = call(
            functools.partial(normals_kernel, chips),
            jax.ShapeDtypeStruct((windows, cell_rows, LANES), F32),
            [smem(), vmem(), vmem()],
            micros=3,
        )(tile_window, w, attitude_partials)
    parts = lax.all_to_all(normals.reshape(devices, own, cell_rows, LANES), "sky", 0, 0, tiled=True)
    _, blocks = lax.optimization_barrier((normals, blocks))
    with jax.named_scope("solve"):
        change, ties = call(
            solve_kernel,
            [
                jax.ShapeDtypeStruct((PARAMS, rows, LANES), F32),
                jax.ShapeDtypeStruct((3, 8, LANES), F32),
            ],
            [smem(), smem()] + [vmem()] * peers,
            [pltpu.VMEM((peers, 8, LANES), F32)],
            micros=30,
        )(me, sky, *blocks)
    changes = swapped([change] * peers)
    with jax.named_scope("invert"):
        inverse = call(
            invert_kernel,
            jax.ShapeDtypeStruct((own, cell_rows, LANES), F32),
            [smem(), vmem(), vmem()],
            [pltpu.VMEM((cell_rows * LANES, LANES), F32), pltpu.VMEM((knots * knots, LANES), F32)],
            micros=3,
        )(sky, parts, ties)
    inverse, changes = lax.optimization_barrier((inverse, changes))
    with jax.named_scope("right_sides"):
        new_sources, part = call(
            functools.partial(rhs_kernel, hi_count),
            [
                jax.ShapeDtypeStruct(sources.shape, F32),
                jax.ShapeDtypeStruct((knots, windows), F32),
            ],
            [smem(), smem()] + [vmem()] * (6 + peers),
            [
                pltpu.VMEM((peers, PARAMS, rows, LANES), F32),
                pltpu.VMEM((SPLITS * PARAMS * hi_count, low_count), F32),
                pltpu.VMEM((low_count, CHUNK), BF16),
                pltpu.VMEM((SPLITS * PARAMS * hi_count, CHUNK), F32),
                pltpu.VMEM((windows, CHUNK), BF16),
            ],
            micros=6,
        )(me, tile_window, src, w, r, source_partials, attitude_partials, sources, *changes)
    with jax.named_scope("send"):
        sides = knots // 2 // 8
        sent = call(
            send_kernel,
            jax.ShapeDtypeStruct((own + sides, 8, LANES), F32),
            [smem()] + [vmem()] * 3,
        )(sky, inverse, part, other_core(part))
    got = [sent] + [
        lax.ppermute(sent, "sky", [(i, i ^ (CORES * k)) for i in range(devices)]) for k in range(1, chips)
    ]
    with jax.named_scope("rims"):
        rim = jax.ShapeDtypeStruct((8 + sides, 8, LANES), F32)
        inner, outer, main = call(
            rim_kernel,
            [rim, rim, jax.ShapeDtypeStruct((HALF + sides, 8, LANES), F32)],
            [smem()] + [vmem()] * chips,
        )(sky, *got)
    upper = [(chip * CORES + 1) * peers + t for chip in range(chips) for t in range(peers - 1)]
    lower = [chip * CORES * peers + t + 1 for chip in range(chips) for t in range(peers - 1)]
    outer = lax.ppermute(outer, ("sky", "tm"), list(zip(upper + lower, lower + upper)))
    inner = other_core(inner)
    with jax.named_scope("sweeps"):
        step = call(
            sweeps_kernel,
            jax.ShapeDtypeStruct((knots, LANES), F32),
            [smem()] + [vmem()] * 4,
            [
                pltpu.VMEM((cell_rows * LANES, LANES), F32),
                pltpu.VMEM((knots * knots, LANES), F32),
                pltpu.VMEM((knots, LANES), F32),
            ],
            micros=1,
        )(sky, main, inner, outer, ties)
    with jax.named_scope("finish"):
        new_attitude = call(
            finish_kernel,
            jax.ShapeDtypeStruct((knots, windows), F32),
            [smem()] + [vmem()] * 3,
        )(sky, step, other_core(step), attitude.T)
    return new_sources, new_attitude.T


def solution(mesh):
    return jax.shard_map(
        on_device,
        mesh=mesh,
        in_specs=(
            P(("sky", "tm")),
            P(("sky", "tm")),
            P(None, ("sky", "tm")),
            P(None, ("sky", "tm")),
            P(("sky", "tm")),
            P(("sky", "tm")),
            P(None, "sky"),
            P("tm", None),
            P("tm"),
        ),
        out_specs=(P(None, "sky"), P("tm", None)),
        check_vma=False,
    )
```

```python
import functools
import math

import jax
import jax.numpy as jnp
from jax import lax
from jax.experimental import pallas as pl
from jax.experimental.pallas import tpu as pltpu
from jax.sharding import PartitionSpec as P

TILE = 128
ITERS = 8
RIM = ITERS - 1
DAMPING = 0.8
PARAMS = 5
PAIRS = tuple((i, j) for i in range(PARAMS) for j in range(i + 1))
MOMENTS = len(PAIRS) + PARAMS
LANES = 128
CORES = 2
HALF = LANES // CORES
SPLITS = 3
ROWS = 8
F32 = jnp.float32
BF16 = jnp.bfloat16
NT = (((1,), (1,)), ((), ()))
FLOPS_MICRO = 1e9
VMEM_LIMIT = 48 * 1024 * 1024


def vmem():
    return pl.BlockSpec(memory_space=pltpu.VMEM)


def smem():
    return pl.BlockSpec(memory_space=pltpu.SMEM)


def call(kernel, out_shape, in_specs, scratch=(), micros=0.1, limit=VMEM_LIMIT):
    return pl.pallas_call(
        kernel,
        out_shape=out_shape,
        in_specs=in_specs,
        out_specs=jax.tree.map(lambda _: vmem(), out_shape),
        scratch_shapes=list(scratch),
        compiler_params=pltpu.CompilerParams(vmem_limit_bytes=limit),
        cost_estimate=pl.CostEstimate(flops=int(micros * FLOPS_MICRO), bytes_accessed=0, transcendentals=0),
    )


def iota(shape, dim):
    return lax.broadcasted_iota(jnp.int32, shape, dim)


def split_bf16(x, parts):
    out = []
    for part in range(parts):
        head = x.astype(BF16)
        out.append(head)
        if part < parts - 1:
            x = x - head.astype(F32)
    return out


def low_one_hot(row, half, low_count):
    low = (row // half) * LANES + (row & (LANES - 1))
    return jnp.where(
        iota((low_count, LANES), 0).astype(F32).astype(BF16) == low.astype(F32).astype(BF16),
        jnp.ones((), BF16),
        jnp.zeros((), BF16),
    )


def high_digit(row, half):
    return (row & (half - 1)) // LANES


def moments_kernel(hi_count, me_ref, src_hbm, w_hbm, r_hbm, sp_hbm, tie_hbm, *refs):
    peers = len(refs) - 10
    outs, (lhs, rhs, acc, blocks, src_ref, w_ref, r_ref, sp_ref, tie_ref, sems) = refs[:peers], refs[peers:]
    pairs = ((src_hbm, src_ref), (w_hbm, w_ref), (r_hbm, r_ref), (sp_hbm, sp_ref), (tie_hbm, tie_ref))
    copies = [pltpu.make_async_copy(a, b, sems.at[i]) for i, (a, b) in enumerate(pairs)]
    for copy in copies:
        copy.start()
    half = hi_count * LANES
    low_count = rhs.shape[0]
    for copy in copies:
        copy.wait()

    tiles = src_ref.shape[0]
    for base in range(0, tiles, ROWS):
        part = slice(base, base + ROWS)
        src, w, r = src_ref[part, :], w_ref[part, :], r_ref[part, :]
        columns = [sp_ref[:, (base + i) * TILE : (base + i + 1) * TILE].astype(F32) for i in range(ROWS)]
        a = [
            jnp.concatenate([columns[i][p : p + 1] for i in range(ROWS)], axis=0)
            for p in range(PARAMS)
        ]
        wa = [w * x for x in a]
        sums = [wa[i] * a[j] for i, j in PAIRS] + [x * r for x in wa]
        parts = [[piece.astype(F32) for piece in split_bf16(s, SPLITS)] for s in sums]
        for i in range(ROWS):
            lanes = slice((base + i) * TILE, (base + i + 1) * TILE)
            row = src[i : i + 1]
            rhs[:, lanes] = low_one_hot(row, half, low_count)
            mask = jnp.where(iota((hi_count, LANES), 0) == high_digit(row, half), 1.0, 0.0).astype(BF16)
            for s in range(SPLITS):
                for p in range(MOMENTS):
                    value = jnp.broadcast_to(parts[p][s][i : i + 1], (hi_count, LANES)).astype(BF16)
                    start = (s * MOMENTS + p) * hi_count
                    lhs[start : start + hi_count, lanes] = value * mask
    acc[...] = lax.dot_general(lhs[...], rhs[...], NT, preferred_element_type=F32)
    rows = blocks.shape[2]
    for p in range(MOMENTS):
        total = acc[p * hi_count : (p + 1) * hi_count, :]
        for s in range(1, SPLITS):
            start = (s * MOMENTS + p) * hi_count
            total = total + acc[start : start + hi_count, :]
        for j in range(peers):
            q, first = divmod(j * rows, hi_count)
            blocks[j, p] = total[first : first + rows, q * LANES : (q + 1) * LANES]
    for j in range(peers):
        blocks[j, MOMENTS] = jnp.broadcast_to(tie_ref[...], (rows, LANES))
    me = me_ref[0]
    for k in range(peers):
        outs[k][...] = blocks[me ^ k]


def normals_kernel(chips, win_ref, w_ref, att_ref, out_ref):
    windows = out_ref.shape[0]
    own = windows // chips // CORES
    knots = att_ref.shape[0]
    copies = LANES // knots
    out_ref[...] = jnp.zeros_like(out_ref)
    blank = jnp.zeros((knots, TILE), BF16)
    lane = iota((8, LANES), 1)

    def pair(u, carry):
        att = att_ref[:, pl.ds(pl.multiple_of(u * 2 * TILE, 2 * TILE), 2 * TILE)]
        w = jnp.concatenate([w_ref[pl.ds(2 * u, 1), :], w_ref[pl.ds(2 * u + 1, 1), :]], axis=1)
        scaled = (w * att.astype(F32)).astype(BF16)
        left = jnp.concatenate([scaled[:, :TILE], blank], axis=1)
        right = jnp.concatenate([blank, scaled[:, TILE:]], axis=1)
        normal = lax.dot_general(
            jnp.concatenate([left, right], axis=0),
            jnp.concatenate([att] * copies, axis=0),
            NT,
            preferred_element_type=F32,
        )
        for h in range(2):
            value = normal[h * knots : h * knots + 8]
            for g in range(1, copies):
                start = h * knots + 8 * g
                value = jnp.where(lane < g * knots, value, normal[start : start + 8])
            slot = lax.rem(win_ref[2 * u + h], windows)
            block = slot // own
            device = lax.rem(block, chips) * CORES + block // chips
            out_ref[device * own + lax.rem(slot, own)] += value
        return carry

    lax.fori_loop(0, w_ref.shape[0] // 2, pair, 0, unroll=True)


def solve_kernel(me_ref, sky_ref, *refs):
    peers = len(refs) - 3
    blocks, (change_ref, ties_ref, rows_scr) = refs[:peers], refs[peers:]
    moments = blocks[0][0:MOMENTS]
    for other in blocks[1:]:
        moments = moments + other[0:MOMENTS]
    matrix = {}
    for position, (i, j) in enumerate(PAIRS):
        matrix[i, j] = moments[position] + (1.0 if i == j else 0.0)
    factor, inverse = {}, {}
    for i in range(PARAMS):
        for j in range(i + 1):
            reduced = matrix[i, j]
            for k in range(j):
                reduced = reduced - factor[i, k] * factor[j, k]
            if i == j:
                factor[i, i] = jnp.sqrt(reduced)
                inverse[i] = 1.0 / factor[i, i]
            else:
                factor[i, j] = reduced * inverse[j]
    forward = []
    for i in range(PARAMS):
        current = moments[len(PAIRS) + i]
        for k in range(i):
            current = current - factor[i, k] * forward[k]
        forward.append(current * inverse[i])
    result = [None] * PARAMS
    for i in reversed(range(PARAMS)):
        current = forward[i]
        for k in range(i + 1, PARAMS):
            current = current - factor[k, i] * result[k]
        result[i] = current * inverse[i]
        change_ref[i] = result[i]
    me, core = me_ref[0], lax.rem(sky_ref[0], CORES)
    for k in range(peers):
        rows_scr[me ^ k] = jnp.broadcast_to(blocks[k][MOMENTS, 0:1, :], (8, LANES))
    first, last = me == 0, me == peers - 1
    own = rows_scr[me]
    before = jnp.where(first, 0.0, rows_scr[jnp.maximum(me - 1, 0)])
    after = jnp.where(last, 0.0, rows_scr[jnp.minimum(me + 1, peers - 1)])
    lane = iota((8, LANES), 1)
    own = jnp.where(jnp.logical_and(last, lane == LANES - 1), 0.0, own)
    own_left = jnp.where(lane == 0, pltpu.roll(before, 1, 1), pltpu.roll(own, 1, 1))
    after_left = jnp.where(lane == 0, pltpu.roll(own, 1, 1), pltpu.roll(after, 1, 1))
    before_left = pltpu.roll(before, 1, 1)
    ties_ref[0] = own_left + own

    def placed(before, own, after):
        low = jnp.where(lane < HALF + RIM, own, jnp.where(lane >= LANES - RIM, before, 0.0))
        high = jnp.where(lane < RIM, after, jnp.where(lane >= HALF - RIM, own, 0.0))
        return jnp.where(core == 0, low, pltpu.roll(high, HALF, 1))

    ties_ref[1] = placed(before_left, own_left, after_left)
    ties_ref[2] = placed(before, own, after)


def invert_kernel(sky_ref, part_ref, ties_ref, out_ref, flat, cells):
    devices, own, _, _ = part_ref.shape
    knots = math.isqrt(out_ref.shape[1] * LANES)
    total = part_ref[0]
    for s in range(1, devices):
        total = total + part_ref[s]
    flat[...] = jnp.zeros_like(flat)
    flat[0 : own * 8, :] = total.reshape(own * 8, LANES)
    groups = LANES // knots
    for r in range(8):
        turned = flat[pl.ds(r, LANES, stride=8), :].T
        for g in range(groups):
            cells[(8 * g + r) * knots : (8 * g + r + 1) * knots, :] = turned[g * knots : (g + 1) * knots]
    core, chip = lax.rem(sky_ref[0], CORES), sky_ref[0] // CORES
    shift = lax.rem(LANES - core * HALF - chip * own, LANES)
    ties = pltpu.roll(ties_ref[0], shift, 1)
    diagonal = jnp.concatenate([ties] * (knots // 8), axis=0)
    inner = iota((knots, LANES), 0)
    blocks = []
    for k in range(knots):
        row = 0.5 * (cells[k * knots : (k + 1) * knots, :] + cells[pl.ds(k, knots, stride=knots), :])
        blocks.append(jnp.where(inner == k, row + diagonal, row))
    for k in range(knots):
        cells[k * knots : (k + 1) * knots, :] = blocks[k]

    def sweep(k, carry):
        at = pl.multiple_of(k * knots, knots)
        row = cells[pl.ds(at, knots), :]
        pivot = 1.0 / cells[pl.ds(at + k, 1), :]
        here = inner == k
        scaled = jnp.where(here, -pivot, row * pivot)
        for i in range(knots):
            old = jnp.where(here, 0.0, cells[i * knots : (i + 1) * knots, :])
            cells[i * knots : (i + 1) * knots, :] = old - row[i : i + 1] * scaled
        cells[pl.ds(at, knots), :] = scaled
        return carry

    lax.fori_loop(0, knots, sweep, 0)
    for r in range(8):
        turned = jnp.concatenate(
            [cells[(8 * g + r) * knots : (8 * g + r + 1) * knots, :] for g in range(groups)], axis=0
        ).T
        flat[pl.ds(r, LANES, stride=8), :] = -turned
    out_ref[...] = flat[0 : own * 8, :].reshape(own, 8, LANES)


def rhs_kernel(hi_count, me_ref, win_ref, src_ref, w_ref, r_ref, sp_ref, att_ref, sources_ref, *refs):
    peers = len(refs) - 7
    blocks = refs[:peers]
    new_ref, out_ref, changes, table, rhs, chosen, weighted = refs[peers:]
    half = hi_count * LANES
    low_count = rhs.shape[0]
    windows = LANES
    me = me_ref[0]
    for k in range(peers):
        changes[me ^ k] = blocks[k][...]
    rows = blocks[0].shape[1]
    for j in range(peers):
        q, first = divmod(j * rows, hi_count)
        for p in range(PARAMS):
            value = changes[j, p]
            for s, piece in enumerate(split_bf16(value, SPLITS)):
                start = (s * PARAMS + p) * hi_count + first
                table[start : start + rows, q * LANES : (q + 1) * LANES] = piece.astype(F32)
        for i in range(rows):
            lanes = slice((j * rows + i) * LANES, (j * rows + i + 1) * LANES)
            step = jnp.concatenate([changes[j, p, i : i + 1, :] for p in range(PARAMS)], axis=0)
            new_ref[:, lanes] = sources_ref[:, lanes] + step
    lookup = table[...].astype(BF16)

    tiles = src_ref.shape[0]
    for i in range(tiles):
        rhs[:, i * TILE : (i + 1) * TILE] = low_one_hot(src_ref[i : i + 1, :], half, low_count)
    chosen[...] = jnp.dot(lookup, rhs[...], preferred_element_type=F32)
    for i in range(tiles):
        lanes = slice(i * TILE, (i + 1) * TILE)
        columns = sp_ref[:, lanes].astype(F32)
        model = jnp.zeros((hi_count, LANES), F32)
        for p in range(PARAMS):
            value = chosen[p * hi_count : (p + 1) * hi_count, lanes]
            for s in range(1, SPLITS):
                start = (s * PARAMS + p) * hi_count
                value = value + chosen[start : start + hi_count, lanes]
            model = model + value * columns[p : p + 1]
        here = iota((hi_count, LANES), 0) == high_digit(src_ref[i : i + 1, :], half)
        model = jnp.sum(jnp.where(here, model, 0.0), axis=0, keepdims=True)
        change = w_ref[i : i + 1, :] * (r_ref[i : i + 1, :] - model)
        slot = lax.rem(win_ref[i], windows)
        weighted[:, lanes] = jnp.where(iota((windows, LANES), 0) == slot, change, 0.0).astype(BF16)
    total = lax.dot_general(att_ref[...], weighted[...], NT, preferred_element_type=F32)
    out_ref[...] = total


def send_kernel(sky_ref, inv_ref, mine_ref, theirs_ref, out_ref):
    own = inv_ref.shape[0]
    core = lax.rem(sky_ref[0], CORES)
    total = mine_ref[...] + theirs_ref[...]
    total = jnp.where(core == 0, total, pltpu.roll(total, HALF, 1))
    packed = narrow(total)
    out_ref[0:own] = inv_ref[...]
    out_ref[own:] = packed.reshape(packed.shape[0] // 8, 8, LANES)


def narrow(x):
    rows = x.shape[0] // 2
    low = iota((rows, LANES), 1) < HALF
    return jnp.where(low, x[:rows], pltpu.roll(x[rows:], HALF, 1))


def widen(x):
    return jnp.concatenate([x, pltpu.roll(x, HALF, 1)], axis=0)


def rim_kernel(sky_ref, *refs):
    chips = len(refs) - 3
    parts, (inner_ref, outer_ref, main_ref) = refs[:chips], refs[chips:]
    own = parts[0].shape[0] - (main_ref.shape[0] - HALF)
    core, chip = lax.rem(sky_ref[0], CORES), sky_ref[0] // CORES
    sides = parts[0][own:]
    for part in parts[1:]:
        sides = sides + part[own:]
    for k in range(chips):
        main_ref[pl.ds((chip ^ k) * own, own)] = parts[k][0:own]
    main_ref[HALF:] = sides
    inner_ref[0:8] = main_ref[pl.ds((1 - core) * (HALF - 8), 8)]
    outer_ref[0:8] = main_ref[pl.ds(core * (HALF - 8), 8)]
    inner_ref[8:] = sides
    outer_ref[8:] = sides


def sweeps_kernel(sky_ref, main_ref, inner_ref, outer_ref, ties_ref, out_ref, flat, cells, vector):
    knots = out_ref.shape[0]
    groups = LANES // knots
    core = lax.rem(sky_ref[0], CORES)
    low = jnp.where(core == 0, outer_ref[...], inner_ref[...])
    high = jnp.where(core == 0, inner_ref[...], outer_ref[...])
    flat[...] = jnp.zeros_like(flat)
    flat[0 : HALF * 8, :] = main_ref[0:HALF].reshape(HALF * 8, LANES)
    flat[HALF * 8 : HALF * 8 + 64, :] = high[0:8].reshape(64, LANES)
    flat[LANES * 8 - 64 : LANES * 8, :] = low[0:8].reshape(64, LANES)
    for r in range(8):
        turned = flat[pl.ds(r, LANES, stride=8), :].T
        for g in range(groups):
            cells[(8 * g + r) * knots : (8 * g + r + 1) * knots, :] = turned[g * knots : (g + 1) * knots]

    def wide(x):
        return widen(x.reshape(knots // 2, LANES))

    lane = iota((knots, LANES), 1)
    sides = jnp.where(lane < HALF, wide(main_ref[HALF:]), 0.0)
    sides = jnp.where(jnp.logical_and(lane >= HALF, lane < HALF + RIM), pltpu.roll(wide(high[8:]), HALF, 1), sides)
    sides = jnp.where(lane >= LANES - RIM, pltpu.roll(wide(low[8:]), HALF, 1), sides)
    left = DAMPING * jnp.concatenate([ties_ref[1]] * (knots // 8), axis=0)
    right = DAMPING * jnp.concatenate([ties_ref[2]] * (knots // 8), axis=0)

    def applied(x):
        vector[...] = x
        total = [jnp.zeros((knots, LANES), F32) for _ in range(4)]
        for k in range(knots):
            total[k % 4] += cells[k * knots : (k + 1) * knots, :] * vector[k : k + 1, :]
        return (total[0] + total[1]) + (total[2] + total[3])

    first = applied(DAMPING * sides)

    def sweep(_, change):
        ends = left * pltpu.roll(change, 1, 1) + right * pltpu.roll(change, LANES - 1, 1)
        return (1.0 - DAMPING) * change + first + applied(ends)

    out_ref[...] = lax.fori_loop(0, ITERS - 1, sweep, first)


def finish_kernel(sky_ref, mine_ref, theirs_ref, attitude_ref, out_ref):
    core = lax.rem(sky_ref[0], CORES)
    lower = jnp.where(core == 0, mine_ref[...], theirs_ref[...])
    upper = jnp.where(core == 0, theirs_ref[...], mine_ref[...])
    lane = iota(lower.shape, 1)
    out_ref[...] = attitude_ref[...] + jnp.where(lane < HALF, lower, pltpu.roll(upper, HALF, 1))


def on_device(
    residuals, weights, source_partials, attitude_partials, source_index, tile_window, sources, attitude, coupling
):
    peers = lax.axis_size("tm")
    devices = lax.axis_size("sky")
    source_count = sources.shape[1]
    windows, knots = attitude.shape
    observations = residuals.shape[0]
    tiles = observations // TILE
    own = windows // devices
    rows = source_count // LANES // peers
    hi_count = source_count // (2 * LANES)
    low_count = 2 * LANES
    me = lax.axis_index("tm").astype(jnp.int32).reshape(1)
    sky = lax.axis_index("sky").astype(jnp.int32).reshape(1)
    src = source_index.reshape(tiles, TILE)
    w = weights.reshape(tiles, TILE)
    r = residuals.reshape(tiles, TILE)

    chips = devices // CORES
    cell_rows = knots * knots // LANES

    def swapped(blocks):
        out = [blocks[0]] + [None] * (peers - 1)
        for k in sorted(range(1, peers), key=lambda k: (k < peers // 2, k)):
            out[k] = lax.ppermute(blocks[k], "tm", [(i, i ^ k) for i in range(peers)])
        return out

    def other_core(x):
        return lax.ppermute(x, "sky", [(i, i ^ 1) for i in range(devices)])

    block = jax.ShapeDtypeStruct((MOMENTS + 1, rows, LANES), F32)
    with jax.named_scope("moments"):
        blocks = call(
            functools.partial(moments_kernel, hi_count),
            [block] * peers,
            [smem()] + [pl.BlockSpec(memory_space=pl.ANY)] * 5,
            [
                pltpu.VMEM((SPLITS * MOMENTS * hi_count, observations), BF16),
                pltpu.VMEM((low_count, observations), BF16),
                pltpu.VMEM((SPLITS * MOMENTS * hi_count, low_count), F32),
                pltpu.VMEM((peers, MOMENTS + 1, rows, LANES), F32),
                pltpu.VMEM(src.shape, jnp.int32),
                pltpu.VMEM(w.shape, F32),
                pltpu.VMEM(r.shape, F32),
                pltpu.VMEM(source_partials.shape, BF16),
                pltpu.VMEM((1, windows), F32),
                pltpu.SemaphoreType.DMA((5,)),
            ],
            micros=7.5,
            limit=60 * 1024 * 1024,
        )(me, src, w, r, source_partials, coupling.reshape(1, windows))
    blocks, tile_window = lax.optimization_barrier((blocks, tile_window))
    blocks = swapped(blocks)
    with jax.named_scope("normals"):
        normals = call(
            functools.partial(normals_kernel, chips),
            jax.ShapeDtypeStruct((windows, cell_rows, LANES), F32),
            [smem(), vmem(), vmem()],
            micros=3,
        )(tile_window, w, attitude_partials)
    parts = lax.all_to_all(normals.reshape(devices, own, cell_rows, LANES), "sky", 0, 0, tiled=True)
    _, blocks = lax.optimization_barrier((normals, blocks))
    with jax.named_scope("solve"):
        change, ties = call(
            solve_kernel,
            [
                jax.ShapeDtypeStruct((PARAMS, rows, LANES), F32),
                jax.ShapeDtypeStruct((3, 8, LANES), F32),
            ],
            [smem(), smem()] + [vmem()] * peers,
            [pltpu.VMEM((peers, 8, LANES), F32)],
            micros=30,
        )(me, sky, *blocks)
    changes = swapped([change] * peers)
    with jax.named_scope("invert"):
        inverse = call(
            invert_kernel,
            jax.ShapeDtypeStruct((own, cell_rows, LANES), F32),
            [smem(), vmem(), vmem()],
            [pltpu.VMEM((cell_rows * LANES, LANES), F32), pltpu.VMEM((knots * knots, LANES), F32)],
            micros=3,
        )(sky, parts, ties)
    inverse, changes = lax.optimization_barrier((inverse, changes))
    with jax.named_scope("right_sides"):
        new_sources, part = call(
            functools.partial(rhs_kernel, hi_count),
            [
                jax.ShapeDtypeStruct(sources.shape, F32),
                jax.ShapeDtypeStruct((knots, windows), F32),
            ],
            [smem(), smem()] + [vmem()] * (6 + peers),
            [
                pltpu.VMEM((peers, PARAMS, rows, LANES), F32),
                pltpu.VMEM((SPLITS * PARAMS * hi_count, low_count), F32),
                pltpu.VMEM((low_count, observations), BF16),
                pltpu.VMEM((SPLITS * PARAMS * hi_count, observations), F32),
                pltpu.VMEM((windows, observations), BF16),
            ],
            micros=6,
        )(me, tile_window, src, w, r, source_partials, attitude_partials, sources, *changes)
    with jax.named_scope("send"):
        sides = knots // 2 // 8
        sent = call(
            send_kernel,
            jax.ShapeDtypeStruct((own + sides, 8, LANES), F32),
            [smem()] + [vmem()] * 3,
        )(sky, inverse, part, other_core(part))
    got = [sent] + [
        lax.ppermute(sent, "sky", [(i, i ^ (CORES * k)) for i in range(devices)]) for k in range(1, chips)
    ]
    with jax.named_scope("rims"):
        rim = jax.ShapeDtypeStruct((8 + sides, 8, LANES), F32)
        inner, outer, main = call(
            rim_kernel,
            [rim, rim, jax.ShapeDtypeStruct((HALF + sides, 8, LANES), F32)],
            [smem()] + [vmem()] * chips,
        )(sky, *got)
    upper = [(chip * CORES + 1) * peers + t for chip in range(chips) for t in range(peers - 1)]
    lower = [chip * CORES * peers + t + 1 for chip in range(chips) for t in range(peers - 1)]
    outer = lax.ppermute(outer, ("sky", "tm"), list(zip(upper + lower, lower + upper)))
    inner = other_core(inner)
    with jax.named_scope("sweeps"):
        step = call(
            sweeps_kernel,
            jax.ShapeDtypeStruct((knots, LANES), F32),
            [smem()] + [vmem()] * 4,
            [
                pltpu.VMEM((cell_rows * LANES, LANES), F32),
                pltpu.VMEM((knots * knots, LANES), F32),
                pltpu.VMEM((knots, LANES), F32),
            ],
            micros=1,
        )(sky, main, inner, outer, ties)
    with jax.named_scope("finish"):
        new_attitude = call(
            finish_kernel,
            jax.ShapeDtypeStruct((knots, windows), F32),
            [smem()] + [vmem()] * 3,
        )(sky, step, other_core(step), attitude.T)
    return new_sources, new_attitude.T


def solution(mesh):
    return jax.shard_map(
        on_device,
        mesh=mesh,
        in_specs=(
            P(("sky", "tm")),
            P(("sky", "tm")),
            P(None, ("sky", "tm")),
            P(None, ("sky", "tm")),
            P(("sky", "tm")),
            P(("sky", "tm")),
            P(None, "sky"),
            P("tm", None),
            P("tm"),
        ),
        out_specs=(P(None, "sky"), P("tm", None)),
        check_vma=False,
    )
```

```python
import functools
import math

import jax
import jax.numpy as jnp
from jax import lax
from jax.experimental import pallas as pl
from jax.experimental.pallas import tpu as pltpu
from jax.sharding import PartitionSpec as P

TILE = 128
ITERS = 8
RIM = ITERS - 1
DAMPING = 0.8
PARAMS = 5
PAIRS = tuple((i, j) for i in range(PARAMS) for j in range(i + 1))
MOMENTS = len(PAIRS) + PARAMS
LANES = 128
CORES = 2
HALF = LANES // CORES
SPLITS = 2
LOOKUP_SPLITS = 3
ROWS = 8
F32 = jnp.float32
BF16 = jnp.bfloat16
NT = (((1,), (1,)), ((), ()))
FLOPS_MICRO = 1e9
VMEM_LIMIT = 48 * 1024 * 1024


def masks(count):
    return [0] + list(range(count - 1, 0, -1))


def vmem():
    return pl.BlockSpec(memory_space=pltpu.VMEM)


def smem():
    return pl.BlockSpec(memory_space=pltpu.SMEM)


def call(kernel, out_shape, in_specs, scratch=(), micros=0.1, limit=VMEM_LIMIT):
    return pl.pallas_call(
        kernel,
        out_shape=out_shape,
        in_specs=in_specs,
        out_specs=jax.tree.map(lambda _: vmem(), out_shape),
        scratch_shapes=list(scratch),
        compiler_params=pltpu.CompilerParams(vmem_limit_bytes=limit),
        cost_estimate=pl.CostEstimate(flops=int(micros * FLOPS_MICRO), bytes_accessed=0, transcendentals=0),
    )


def iota(shape, dim):
    return lax.broadcasted_iota(jnp.int32, shape, dim)


def split_bf16(x, parts):
    out = []
    for part in range(parts):
        head = x.astype(BF16)
        out.append(head)
        if part < parts - 1:
            x = x - head.astype(F32)
    return out


def low_one_hot(row, half, low_count):
    low = (row // half) * LANES + (row & (LANES - 1))
    return jnp.where(
        iota((low_count, LANES), 0).astype(F32).astype(BF16) == low.astype(F32).astype(BF16),
        jnp.ones((), BF16),
        jnp.zeros((), BF16),
    )


def high_digit(row, half):
    return (row & (half - 1)) // LANES


def sums_kernel(hi_count, me_ref, sky_ref, win_ref, src_hbm, w_hbm, r_hbm, sp_hbm, att_hbm, tie_hbm, *refs):
    peers = len(refs) - 14
    outs, (keep_ref, give_ref, normals, lhs, rhs, acc, blocks) = refs[:peers], refs[peers : peers + 7]
    src_ref, w_ref, r_ref, sp_ref, att_ref, tie_ref, sems = refs[peers + 7 :]
    pairs = (
        (w_hbm, w_ref),
        (att_hbm, att_ref),
        (src_hbm, src_ref),
        (r_hbm, r_ref),
        (sp_hbm, sp_ref),
        (tie_hbm, tie_ref),
    )
    copies = [pltpu.make_async_copy(a, b, sems.at[i]) for i, (a, b) in enumerate(pairs)]
    for copy in copies:
        copy.start()
    normals[...] = jnp.zeros_like(normals)
    for copy in copies[:2]:
        copy.wait()
    window_normals(win_ref, w_ref, att_ref, normals)
    core = lax.rem(sky_ref[0], CORES)
    keep_ref[...] = normals[pl.ds(core * HALF, HALF)]
    give_ref[...] = normals[pl.ds((1 - core) * HALF, HALF)]
    for copy in copies[2:]:
        copy.wait()
    half = hi_count * LANES
    low_count = rhs.shape[0]
    tiles = src_ref.shape[0]
    for base in range(0, tiles, ROWS):
        part = slice(base, base + ROWS)
        src, w, r = src_ref[part, :], w_ref[part, :], r_ref[part, :]
        columns = [sp_ref[:, (base + i) * TILE : (base + i + 1) * TILE].astype(F32) for i in range(ROWS)]
        a = [
            jnp.concatenate([columns[i][p : p + 1] for i in range(ROWS)], axis=0)
            for p in range(PARAMS)
        ]
        wa = [w * x for x in a]
        sums = [wa[i] * a[j] for i, j in PAIRS] + [x * r for x in wa]
        parts = [[piece.astype(F32) for piece in split_bf16(s, SPLITS)] for s in sums]
        for i in range(ROWS):
            lanes = slice((base + i) * TILE, (base + i + 1) * TILE)
            row = src[i : i + 1]
            rhs[:, lanes] = low_one_hot(row, half, low_count)
            mask = jnp.where(iota((hi_count, LANES), 0) == high_digit(row, half), 1.0, 0.0).astype(BF16)
            for s in range(SPLITS):
                for p in range(MOMENTS):
                    value = jnp.broadcast_to(parts[p][s][i : i + 1], (hi_count, LANES)).astype(BF16)
                    start = (s * MOMENTS + p) * hi_count
                    lhs[start : start + hi_count, lanes] = value * mask
    acc[...] = lax.dot_general(lhs[...], rhs[...], NT, preferred_element_type=F32)
    rows = blocks.shape[2]
    for p in range(MOMENTS):
        total = acc[p * hi_count : (p + 1) * hi_count, :]
        for s in range(1, SPLITS):
            start = (s * MOMENTS + p) * hi_count
            total = total + acc[start : start + hi_count, :]
        for j in range(peers):
            q, first = divmod(j * rows, hi_count)
            blocks[j, p] = total[first : first + rows, q * LANES : (q + 1) * LANES]
    for j in range(peers):
        blocks[j, MOMENTS] = jnp.broadcast_to(tie_ref[...], (rows, LANES))
    me = me_ref[0]
    for out, mask in zip(outs, masks(peers)):
        out[...] = blocks[me ^ mask]


def window_normals(win_ref, w_ref, att_ref, sums):
    windows = sums.shape[0]
    knots = att_ref.shape[0]
    copies = LANES // knots
    blank = jnp.zeros((knots, TILE), BF16)
    lane = iota((8, LANES), 1)

    for u in range(w_ref.shape[0] // 2):
        att = att_ref[:, 2 * u * TILE : 2 * (u + 1) * TILE]
        w = jnp.concatenate([w_ref[2 * u : 2 * u + 1, :], w_ref[2 * u + 1 : 2 * u + 2, :]], axis=1)
        scaled = (w * att.astype(F32)).astype(BF16)
        left = jnp.concatenate([scaled[:, :TILE], blank], axis=1)
        right = jnp.concatenate([blank, scaled[:, TILE:]], axis=1)
        normal = lax.dot_general(
            jnp.concatenate([left, right], axis=0),
            jnp.concatenate([att] * copies, axis=0),
            NT,
            preferred_element_type=F32,
        )
        for h in range(2):
            value = normal[h * knots : h * knots + 8]
            for g in range(1, copies):
                start = h * knots + 8 * g
                value = jnp.where(lane < g * knots, value, normal[start : start + 8])
            sums[lax.rem(win_ref[2 * u + h], windows)] += value


def halves_kernel(sky_ref, keep_ref, got_ref, *refs):
    outs, total = refs[:-1], refs[-1]
    chip = sky_ref[0] // CORES
    own = outs[0].shape[0]
    total[...] = keep_ref[...] + got_ref[...]
    for out_ref, mask in zip(outs, masks(len(outs))):
        out_ref[...] = total[pl.ds((chip ^ mask) * own, own)]


def solve_kernel(me_ref, sky_ref, *refs):
    peers = len(refs) - 3
    blocks, (change_ref, ties_ref, rows_scr) = refs[:peers], refs[peers:]
    moments = blocks[0][0:MOMENTS]
    for other in blocks[1:]:
        moments = moments + other[0:MOMENTS]
    matrix = {}
    for position, (i, j) in enumerate(PAIRS):
        matrix[i, j] = moments[position] + (1.0 if i == j else 0.0)
    factor, inverse = {}, {}
    for i in range(PARAMS):
        for j in range(i + 1):
            reduced = matrix[i, j]
            for k in range(j):
                reduced = reduced - factor[i, k] * factor[j, k]
            if i == j:
                factor[i, i] = jnp.sqrt(reduced)
                inverse[i] = 1.0 / factor[i, i]
            else:
                factor[i, j] = reduced * inverse[j]
    forward = []
    for i in range(PARAMS):
        current = moments[len(PAIRS) + i]
        for k in range(i):
            current = current - factor[i, k] * forward[k]
        forward.append(current * inverse[i])
    result = [None] * PARAMS
    for i in reversed(range(PARAMS)):
        current = forward[i]
        for k in range(i + 1, PARAMS):
            current = current - factor[k, i] * result[k]
        result[i] = current * inverse[i]
        change_ref[i] = result[i]
    me, core = me_ref[0], lax.rem(sky_ref[0], CORES)
    for block, mask in zip(blocks, masks(peers)):
        rows_scr[me ^ mask] = jnp.broadcast_to(block[MOMENTS, 0:1, :], (8, LANES))
    first, last = me == 0, me == peers - 1
    own = rows_scr[me]
    before = jnp.where(first, 0.0, rows_scr[jnp.maximum(me - 1, 0)])
    after = jnp.where(last, 0.0, rows_scr[jnp.minimum(me + 1, peers - 1)])
    lane = iota((8, LANES), 1)
    own = jnp.where(jnp.logical_and(last, lane == LANES - 1), 0.0, own)
    own_left = jnp.where(lane == 0, pltpu.roll(before, 1, 1), pltpu.roll(own, 1, 1))
    after_left = jnp.where(lane == 0, pltpu.roll(own, 1, 1), pltpu.roll(after, 1, 1))
    before_left = pltpu.roll(before, 1, 1)
    ties_ref[0] = own_left + own

    def placed(before, own, after):
        low = jnp.where(lane < HALF + RIM, own, jnp.where(lane >= LANES - RIM, before, 0.0))
        high = jnp.where(lane < RIM, after, jnp.where(lane >= HALF - RIM, own, 0.0))
        return jnp.where(core == 0, low, pltpu.roll(high, HALF, 1))

    ties_ref[1] = placed(before_left, own_left, after_left)
    ties_ref[2] = placed(before, own, after)


def invert_kernel(sky_ref, ties_ref, *refs):
    parts, (out_ref, flat, cells) = refs[:-3], refs[-3:]
    own = out_ref.shape[0]
    knots = math.isqrt(out_ref.shape[1] * LANES)
    total = parts[0][...]
    for part in parts[1:]:
        total = total + part[...]
    flat[...] = jnp.zeros_like(flat)
    flat[0 : own * 8, :] = total.reshape(own * 8, LANES)
    groups = LANES // knots
    for r in range(8):
        turned = flat[pl.ds(r, LANES, stride=8), :].T
        for g in range(groups):
            cells[(8 * g + r) * knots : (8 * g + r + 1) * knots, :] = turned[g * knots : (g + 1) * knots]
    core, chip = lax.rem(sky_ref[0], CORES), sky_ref[0] // CORES
    shift = lax.rem(LANES - core * HALF - chip * own, LANES)
    ties = pltpu.roll(ties_ref[0], shift, 1)
    diagonal = jnp.concatenate([ties] * (knots // 8), axis=0)
    inner = iota((knots, LANES), 0)
    blocks = []
    for k in range(knots):
        row = 0.5 * (cells[k * knots : (k + 1) * knots, :] + cells[pl.ds(k, knots, stride=knots), :])
        blocks.append(jnp.where(inner == k, row + diagonal, row))
    for k in range(knots):
        cells[k * knots : (k + 1) * knots, :] = blocks[k]

    def sweep(k, carry):
        at = pl.multiple_of(k * knots, knots)
        row = cells[pl.ds(at, knots), :]
        pivot = 1.0 / cells[pl.ds(at + k, 1), :]
        here = inner == k
        scaled = jnp.where(here, -pivot, row * pivot)
        for i in range(knots):
            old = jnp.where(here, 0.0, cells[i * knots : (i + 1) * knots, :])
            cells[i * knots : (i + 1) * knots, :] = old - row[i : i + 1] * scaled
        cells[pl.ds(at, knots), :] = scaled
        return carry

    lax.fori_loop(0, knots, sweep, 0)
    for r in range(8):
        turned = jnp.concatenate(
            [cells[(8 * g + r) * knots : (8 * g + r + 1) * knots, :] for g in range(groups)], axis=0
        ).T
        flat[pl.ds(r, LANES, stride=8), :] = -turned
    out_ref[...] = flat[0 : own * 8, :].reshape(own, 8, LANES)


def low_kernel(half, src_ref, out_ref):
    for i in range(src_ref.shape[0]):
        out_ref[:, i * TILE : (i + 1) * TILE] = low_one_hot(src_ref[i : i + 1, :], half, out_ref.shape[0])


def rhs_kernel(hi_count, me_ref, win_ref, low_ref, src_ref, w_ref, r_ref, sp_ref, att_ref, sources_ref, *refs):
    peers = len(refs) - 6
    blocks = refs[:peers]
    new_ref, out_ref, changes, table, chosen, weighted = refs[peers:]
    half = hi_count * LANES
    windows = LANES
    me = me_ref[0]
    for block, mask in zip(blocks, masks(peers)):
        changes[me ^ mask] = block[...]
    rows = blocks[0].shape[1]
    for j in range(peers):
        q, first = divmod(j * rows, hi_count)
        for p in range(PARAMS):
            value = changes[j, p]
            for s, piece in enumerate(split_bf16(value, LOOKUP_SPLITS)):
                start = (s * PARAMS + p) * hi_count + first
                table[start : start + rows, q * LANES : (q + 1) * LANES] = piece.astype(F32)
        for i in range(rows):
            lanes = slice((j * rows + i) * LANES, (j * rows + i + 1) * LANES)
            step = jnp.concatenate([changes[j, p, i : i + 1, :] for p in range(PARAMS)], axis=0)
            new_ref[:, lanes] = sources_ref[:, lanes] + step
    lookup = table[...].astype(BF16)

    tiles = src_ref.shape[0]
    window_ids = iota((windows, LANES), 0).astype(F32).astype(BF16)
    chosen[...] = jnp.dot(lookup, low_ref[...], preferred_element_type=F32)
    for i in range(tiles):
        lanes = slice(i * TILE, (i + 1) * TILE)
        columns = sp_ref[:, lanes].astype(F32)
        model = jnp.zeros((hi_count, LANES), F32)
        for p in range(PARAMS):
            value = chosen[p * hi_count : (p + 1) * hi_count, lanes]
            for s in range(1, LOOKUP_SPLITS):
                start = (s * PARAMS + p) * hi_count
                value = value + chosen[start : start + hi_count, lanes]
            model = model + value * columns[p : p + 1]
        here = iota((hi_count, LANES), 0) == high_digit(src_ref[i : i + 1, :], half)
        model = jnp.sum(jnp.where(here, model, 0.0), axis=0, keepdims=True)
        change = w_ref[i : i + 1, :] * (r_ref[i : i + 1, :] - model)
        slot = lax.rem(win_ref[i], windows).astype(F32).astype(BF16)
        change = jnp.broadcast_to(change, (windows, LANES)).astype(BF16)
        weighted[:, lanes] = jnp.where(window_ids == slot, change, jnp.zeros((), BF16))
    total = lax.dot_general(att_ref[...], weighted[...], NT, preferred_element_type=F32)
    out_ref[...] = total


def send_kernel(sky_ref, inv_ref, mine_ref, theirs_ref, out_ref):
    own = inv_ref.shape[0]
    core = lax.rem(sky_ref[0], CORES)
    total = mine_ref[...] + theirs_ref[...]
    total = jnp.where(core == 0, total, pltpu.roll(total, HALF, 1))
    packed = narrow(total)
    out_ref[0:own] = inv_ref[...]
    out_ref[own:] = packed.reshape(packed.shape[0] // 8, 8, LANES)


def narrow(x):
    rows = x.shape[0] // 2
    low = iota((rows, LANES), 1) < HALF
    return jnp.where(low, x[:rows], pltpu.roll(x[rows:], HALF, 1))


def widen(x):
    return jnp.concatenate([x, pltpu.roll(x, HALF, 1)], axis=0)


def rim_kernel(sky_ref, *refs):
    chips = len(refs) - 3
    parts, (inner_ref, outer_ref, main_ref) = refs[:chips], refs[chips:]
    own = parts[0].shape[0] - (main_ref.shape[0] - HALF)
    core, chip = lax.rem(sky_ref[0], CORES), sky_ref[0] // CORES
    sides = parts[0][own:]
    for part in parts[1:]:
        sides = sides + part[own:]
    for part, mask in zip(parts, masks(chips)):
        main_ref[pl.ds((chip ^ mask) * own, own)] = part[0:own]
    main_ref[HALF:] = sides
    inner_ref[0:8] = main_ref[pl.ds((1 - core) * (HALF - 8), 8)]
    outer_ref[0:8] = main_ref[pl.ds(core * (HALF - 8), 8)]
    inner_ref[8:] = sides
    outer_ref[8:] = sides


def sweeps_kernel(sky_ref, main_ref, inner_ref, outer_ref, ties_ref, out_ref, flat, cells, vector):
    knots = out_ref.shape[0]
    groups = LANES // knots
    core = lax.rem(sky_ref[0], CORES)
    low = jnp.where(core == 0, outer_ref[...], inner_ref[...])
    high = jnp.where(core == 0, inner_ref[...], outer_ref[...])
    flat[...] = jnp.zeros_like(flat)
    flat[0 : HALF * 8, :] = main_ref[0:HALF].reshape(HALF * 8, LANES)
    flat[HALF * 8 : HALF * 8 + 64, :] = high[0:8].reshape(64, LANES)
    flat[LANES * 8 - 64 : LANES * 8, :] = low[0:8].reshape(64, LANES)
    for r in range(8):
        turned = flat[pl.ds(r, LANES, stride=8), :].T
        for g in range(groups):
            cells[(8 * g + r) * knots : (8 * g + r + 1) * knots, :] = turned[g * knots : (g + 1) * knots]

    def wide(x):
        return widen(x.reshape(knots // 2, LANES))

    lane = iota((knots, LANES), 1)
    sides = jnp.where(lane < HALF, wide(main_ref[HALF:]), 0.0)
    sides = jnp.where(jnp.logical_and(lane >= HALF, lane < HALF + RIM), pltpu.roll(wide(high[8:]), HALF, 1), sides)
    sides = jnp.where(lane >= LANES - RIM, pltpu.roll(wide(low[8:]), HALF, 1), sides)
    left = DAMPING * jnp.concatenate([ties_ref[1]] * (knots // 8), axis=0)
    right = DAMPING * jnp.concatenate([ties_ref[2]] * (knots // 8), axis=0)

    def applied(x):
        vector[...] = x
        total = [jnp.zeros((knots, LANES), F32) for _ in range(4)]
        for k in range(knots):
            total[k % 4] += cells[k * knots : (k + 1) * knots, :] * vector[k : k + 1, :]
        return (total[0] + total[1]) + (total[2] + total[3])

    first = applied(DAMPING * sides)

    def sweep(_, change):
        ends = left * pltpu.roll(change, 1, 1) + right * pltpu.roll(change, LANES - 1, 1)
        return (1.0 - DAMPING) * change + first + applied(ends)

    out_ref[...] = lax.fori_loop(0, ITERS - 1, sweep, first)


def finish_kernel(sky_ref, mine_ref, theirs_ref, attitude_ref, out_ref):
    core = lax.rem(sky_ref[0], CORES)
    lower = jnp.where(core == 0, mine_ref[...], theirs_ref[...])
    upper = jnp.where(core == 0, theirs_ref[...], mine_ref[...])
    lane = iota(lower.shape, 1)
    out_ref[...] = attitude_ref[...] + jnp.where(lane < HALF, lower, pltpu.roll(upper, HALF, 1))


def on_device(
    residuals, weights, source_partials, attitude_partials, source_index, tile_window, sources, attitude, coupling
):
    peers = lax.axis_size("tm")
    devices = lax.axis_size("sky")
    source_count = sources.shape[1]
    windows, knots = attitude.shape
    observations = residuals.shape[0]
    tiles = observations // TILE
    own = windows // devices
    rows = source_count // LANES // peers
    hi_count = source_count // (2 * LANES)
    low_count = 2 * LANES
    me = lax.axis_index("tm").astype(jnp.int32).reshape(1)
    sky = lax.axis_index("sky").astype(jnp.int32).reshape(1)
    src = source_index.reshape(tiles, TILE)
    w = weights.reshape(tiles, TILE)
    r = residuals.reshape(tiles, TILE)

    chips = devices // CORES
    cell_rows = knots * knots // LANES

    def swapped(blocks):
        return [blocks[0]] + [
            lax.ppermute(block, "tm", [(i, i ^ mask) for i in range(peers)])
            for block, mask in zip(blocks[1:], masks(peers)[1:])
        ]

    def other_core(x):
        return lax.ppermute(x, "sky", [(i, i ^ 1) for i in range(devices)])

    def other_chips(blocks):
        return [blocks[0]] + [
            lax.ppermute(block, "sky", [(i, i ^ (CORES * mask)) for i in range(devices)])
            for block, mask in zip(blocks[1:], masks(chips)[1:])
        ]

    block = jax.ShapeDtypeStruct((MOMENTS + 1, rows, LANES), F32)
    half = jax.ShapeDtypeStruct((HALF, cell_rows, LANES), F32)
    with jax.named_scope("sums"):
        *blocks, keep, give = call(
            functools.partial(sums_kernel, hi_count),
            [block] * peers + [half] * 2,
            [smem()] * 3 + [pl.BlockSpec(memory_space=pl.ANY)] * 6,
            [
                pltpu.VMEM((windows, cell_rows, LANES), F32),
                pltpu.VMEM((SPLITS * MOMENTS * hi_count, observations), BF16),
                pltpu.VMEM((low_count, observations), BF16),
                pltpu.VMEM((SPLITS * MOMENTS * hi_count, low_count), F32),
                pltpu.VMEM((peers, MOMENTS + 1, rows, LANES), F32),
                pltpu.VMEM(src.shape, jnp.int32),
                pltpu.VMEM(w.shape, F32),
                pltpu.VMEM(r.shape, F32),
                pltpu.VMEM(source_partials.shape, BF16),
                pltpu.VMEM(attitude_partials.shape, BF16),
                pltpu.VMEM((1, windows), F32),
                pltpu.SemaphoreType.DMA((6,)),
            ],
            micros=9,
            limit=60 * 1024 * 1024,
        )(me, sky, tile_window, src, w, r, source_partials, attitude_partials, coupling.reshape(1, windows))
    blocks, after_sums = lax.optimization_barrier((blocks, src))
    blocks = swapped(blocks)
    with jax.named_scope("halves"):
        parts = call(
            halves_kernel,
            [jax.ShapeDtypeStruct((own, cell_rows, LANES), F32)] * chips,
            [smem(), vmem(), vmem()],
            [pltpu.VMEM((HALF, cell_rows, LANES), F32)],
        )(sky, keep, other_core(give))
    with jax.named_scope("one_hot"):
        low = call(
            functools.partial(low_kernel, hi_count * LANES),
            jax.ShapeDtypeStruct((low_count, observations), BF16),
            [vmem()],
            micros=1,
        )(after_sums)
    _, low, blocks = lax.optimization_barrier((parts, low, blocks))
    parts = other_chips(parts)
    with jax.named_scope("solve"):
        change, ties = call(
            solve_kernel,
            [
                jax.ShapeDtypeStruct((PARAMS, rows, LANES), F32),
                jax.ShapeDtypeStruct((3, 8, LANES), F32),
            ],
            [smem(), smem()] + [vmem()] * peers,
            [pltpu.VMEM((peers, 8, LANES), F32)],
            micros=30,
        )(me, sky, *blocks)
    changes = swapped([change] * peers)
    with jax.named_scope("invert"):
        inverse = call(
            invert_kernel,
            jax.ShapeDtypeStruct((own, cell_rows, LANES), F32),
            [smem()] + [vmem()] * (1 + chips),
            [pltpu.VMEM((cell_rows * LANES, LANES), F32), pltpu.VMEM((knots * knots, LANES), F32)],
            micros=3,
        )(sky, ties, *parts)
    inverse, changes = lax.optimization_barrier((inverse, changes))
    with jax.named_scope("right_sides"):
        new_sources, part = call(
            functools.partial(rhs_kernel, hi_count),
            [
                jax.ShapeDtypeStruct(sources.shape, F32),
                jax.ShapeDtypeStruct((knots, windows), F32),
            ],
            [smem(), smem()] + [vmem()] * (7 + peers),
            [
                pltpu.VMEM((peers, PARAMS, rows, LANES), F32),
                pltpu.VMEM((LOOKUP_SPLITS * PARAMS * hi_count, low_count), F32),
                pltpu.VMEM((LOOKUP_SPLITS * PARAMS * hi_count, observations), F32),
                pltpu.VMEM((windows, observations), BF16),
            ],
            micros=6,
        )(me, tile_window, low, src, w, r, source_partials, attitude_partials, sources, *changes)
    with jax.named_scope("send"):
        sides = knots // 2 // 8
        sent = call(
            send_kernel,
            jax.ShapeDtypeStruct((own + sides, 8, LANES), F32),
            [smem()] + [vmem()] * 3,
        )(sky, inverse, part, other_core(part))
    got = other_chips([sent] * chips)
    with jax.named_scope("rims"):
        rim = jax.ShapeDtypeStruct((8 + sides, 8, LANES), F32)
        inner, outer, main = call(
            rim_kernel,
            [rim, rim, jax.ShapeDtypeStruct((HALF + sides, 8, LANES), F32)],
            [smem()] + [vmem()] * chips,
        )(sky, *got)
    upper = [(chip * CORES + 1) * peers + t for chip in range(chips) for t in range(peers - 1)]
    lower = [chip * CORES * peers + t + 1 for chip in range(chips) for t in range(peers - 1)]
    outer = lax.ppermute(outer, ("sky", "tm"), list(zip(upper + lower, lower + upper)))
    inner = other_core(inner)
    with jax.named_scope("sweeps"):
        step = call(
            sweeps_kernel,
            jax.ShapeDtypeStruct((knots, LANES), F32),
            [smem()] + [vmem()] * 4,
            [
                pltpu.VMEM((cell_rows * LANES, LANES), F32),
                pltpu.VMEM((knots * knots, LANES), F32),
                pltpu.VMEM((knots, LANES), F32),
            ],
            micros=1,
        )(sky, main, inner, outer, ties)
    with jax.named_scope("finish"):
        new_attitude = call(
            finish_kernel,
            jax.ShapeDtypeStruct((knots, windows), F32),
            [smem()] + [vmem()] * 3,
        )(sky, step, other_core(step), attitude.T)
    return new_sources, new_attitude.T


def solution(mesh):
    return jax.shard_map(
        on_device,
        mesh=mesh,
        in_specs=(
            P(("sky", "tm")),
            P(("sky", "tm")),
            P(None, ("sky", "tm")),
            P(None, ("sky", "tm")),
            P(("sky", "tm")),
            P(("sky", "tm")),
            P(None, "sky"),
            P("tm", None),
            P("tm"),
        ),
        out_specs=(P(None, "sky"), P("tm", None)),
        check_vma=False,
    )
```

```python
import functools
import math

import jax
import jax.numpy as jnp
from jax import lax
from jax.experimental import pallas as pl
from jax.experimental.pallas import tpu as pltpu
from jax.sharding import PartitionSpec as P

TILE = 128
ITERS = 8
RIM = ITERS - 1
DAMPING = 0.8
PARAMS = 5
PAIRS = tuple((i, j) for i in range(PARAMS) for j in range(i + 1))
MOMENTS = len(PAIRS) + PARAMS
LANES = 128
CORES = 2
HALF = LANES // CORES
SPLITS = 2
ROWS = 8
F32 = jnp.float32
BF16 = jnp.bfloat16
NT = (((1,), (1,)), ((), ()))
FLOPS_MICRO = 1e9
VMEM_LIMIT = 48 * 1024 * 1024


def masks(count):
    return [0] + list(range(count - 1, 0, -1))


def vmem():
    return pl.BlockSpec(memory_space=pltpu.VMEM)


def smem():
    return pl.BlockSpec(memory_space=pltpu.SMEM)


def call(kernel, out_shape, in_specs, scratch=(), micros=0.1, limit=VMEM_LIMIT):
    return pl.pallas_call(
        kernel,
        out_shape=out_shape,
        in_specs=in_specs,
        out_specs=jax.tree.map(lambda _: vmem(), out_shape),
        scratch_shapes=list(scratch),
        compiler_params=pltpu.CompilerParams(vmem_limit_bytes=limit),
        cost_estimate=pl.CostEstimate(flops=int(micros * FLOPS_MICRO), bytes_accessed=0, transcendentals=0),
    )


def iota(shape, dim):
    return lax.broadcasted_iota(jnp.int32, shape, dim)


def split_bf16(x, parts):
    out = []
    for part in range(parts):
        head = x.astype(BF16)
        out.append(head)
        if part < parts - 1:
            x = x - head.astype(F32)
    return out


def low_one_hot(row, half, low_count):
    low = (row // half) * LANES + (row & (LANES - 1))
    return jnp.where(
        iota((low_count, LANES), 0).astype(F32).astype(BF16) == low.astype(F32).astype(BF16),
        jnp.ones((), BF16),
        jnp.zeros((), BF16),
    )


def high_digit(row, half):
    return (row & (half - 1)) // LANES


def sums_kernel(hi_count, me_ref, sky_ref, win_ref, src_hbm, w_hbm, r_hbm, sp_hbm, att_hbm, tie_hbm, *refs):
    peers = len(refs) - 14
    outs, (keep_ref, give_ref, normals, lhs, rhs, acc, blocks) = refs[:peers], refs[peers : peers + 7]
    src_ref, w_ref, r_ref, sp_ref, att_ref, tie_ref, sems = refs[peers + 7 :]
    pairs = (
        (w_hbm, w_ref),
        (att_hbm, att_ref),
        (src_hbm, src_ref),
        (r_hbm, r_ref),
        (sp_hbm, sp_ref),
        (tie_hbm, tie_ref),
    )
    copies = [pltpu.make_async_copy(a, b, sems.at[i]) for i, (a, b) in enumerate(pairs)]
    for copy in copies:
        copy.start()
    normals[...] = jnp.zeros_like(normals)
    for copy in copies[:2]:
        copy.wait()
    window_normals(win_ref, w_ref, att_ref, normals)
    core = lax.rem(sky_ref[0], CORES)
    keep_ref[...] = normals[pl.ds(core * HALF, HALF)]
    give_ref[...] = normals[pl.ds((1 - core) * HALF, HALF)]
    for copy in copies[2:]:
        copy.wait()
    half = hi_count * LANES
    low_count = rhs.shape[0]
    tiles = src_ref.shape[0]
    for base in range(0, tiles, ROWS):
        part = slice(base, base + ROWS)
        src, w, r = src_ref[part, :], w_ref[part, :], r_ref[part, :]
        columns = [sp_ref[:, (base + i) * TILE : (base + i + 1) * TILE].astype(F32) for i in range(ROWS)]
        a = [
            jnp.concatenate([columns[i][p : p + 1] for i in range(ROWS)], axis=0)
            for p in range(PARAMS)
        ]
        wa = [w * x for x in a]
        sums = [wa[i] * a[j] for i, j in PAIRS] + [x * r for x in wa]
        parts = [[piece.astype(F32) for piece in split_bf16(s, SPLITS)] for s in sums]
        for i in range(ROWS):
            lanes = slice((base + i) * TILE, (base + i + 1) * TILE)
            row = src[i : i + 1]
            rhs[:, lanes] = low_one_hot(row, half, low_count)
            mask = jnp.where(iota((hi_count, LANES), 0) == high_digit(row, half), 1.0, 0.0).astype(BF16)
            for s in range(SPLITS):
                for p in range(MOMENTS):
                    value = jnp.broadcast_to(parts[p][s][i : i + 1], (hi_count, LANES)).astype(BF16)
                    start = (s * MOMENTS + p) * hi_count
                    lhs[start : start + hi_count, lanes] = value * mask
    acc[...] = lax.dot_general(lhs[...], rhs[...], NT, preferred_element_type=F32)
    rows = blocks.shape[2]
    for p in range(MOMENTS):
        total = acc[p * hi_count : (p + 1) * hi_count, :]
        for s in range(1, SPLITS):
            start = (s * MOMENTS + p) * hi_count
            total = total + acc[start : start + hi_count, :]
        for j in range(peers):
            q, first = divmod(j * rows, hi_count)
            blocks[j, p] = total[first : first + rows, q * LANES : (q + 1) * LANES]
    for j in range(peers):
        blocks[j, MOMENTS] = jnp.broadcast_to(tie_ref[...], (rows, LANES))
    me = me_ref[0]
    for out, mask in zip(outs, masks(peers)):
        out[...] = blocks[me ^ mask]


def window_normals(win_ref, w_ref, att_ref, sums):
    windows = sums.shape[0]
    knots = att_ref.shape[0]
    copies = LANES // knots
    blank = jnp.zeros((knots, TILE), BF16)
    lane = iota((8, LANES), 1)

    for u in range(w_ref.shape[0] // 2):
        att = att_ref[:, 2 * u * TILE : 2 * (u + 1) * TILE]
        w = jnp.concatenate([w_ref[2 * u : 2 * u + 1, :], w_ref[2 * u + 1 : 2 * u + 2, :]], axis=1)
        scaled = (w * att.astype(F32)).astype(BF16)
        left = jnp.concatenate([scaled[:, :TILE], blank], axis=1)
        right = jnp.concatenate([blank, scaled[:, TILE:]], axis=1)
        normal = lax.dot_general(
            jnp.concatenate([left, right], axis=0),
            jnp.concatenate([att] * copies, axis=0),
            NT,
            preferred_element_type=F32,
        )
        for h in range(2):
            value = normal[h * knots : h * knots + 8]
            for g in range(1, copies):
                start = h * knots + 8 * g
                value = jnp.where(lane < g * knots, value, normal[start : start + 8])
            sums[lax.rem(win_ref[2 * u + h], windows)] += value


def halves_kernel(sky_ref, keep_ref, got_ref, *refs):
    outs, total = refs[:-1], refs[-1]
    chip = sky_ref[0] // CORES
    own = outs[0].shape[0]
    total[...] = keep_ref[...] + got_ref[...]
    for out_ref, mask in zip(outs, masks(len(outs))):
        out_ref[...] = total[pl.ds((chip ^ mask) * own, own)]


def solve_kernel(me_ref, sky_ref, *refs):
    peers = len(refs) - 3
    blocks, (change_ref, ties_ref, rows_scr) = refs[:peers], refs[peers:]
    moments = blocks[0][0:MOMENTS]
    for other in blocks[1:]:
        moments = moments + other[0:MOMENTS]
    matrix = {}
    for position, (i, j) in enumerate(PAIRS):
        matrix[i, j] = moments[position] + (1.0 if i == j else 0.0)
    factor, inverse = {}, {}
    for i in range(PARAMS):
        for j in range(i + 1):
            reduced = matrix[i, j]
            for k in range(j):
                reduced = reduced - factor[i, k] * factor[j, k]
            if i == j:
                factor[i, i] = jnp.sqrt(reduced)
                inverse[i] = 1.0 / factor[i, i]
            else:
                factor[i, j] = reduced * inverse[j]
    forward = []
    for i in range(PARAMS):
        current = moments[len(PAIRS) + i]
        for k in range(i):
            current = current - factor[i, k] * forward[k]
        forward.append(current * inverse[i])
    result = [None] * PARAMS
    for i in reversed(range(PARAMS)):
        current = forward[i]
        for k in range(i + 1, PARAMS):
            current = current - factor[k, i] * result[k]
        result[i] = current * inverse[i]
        change_ref[i] = result[i]
    me, core = me_ref[0], lax.rem(sky_ref[0], CORES)
    for block, mask in zip(blocks, masks(peers)):
        rows_scr[me ^ mask] = jnp.broadcast_to(block[MOMENTS, 0:1, :], (8, LANES))
    first, last = me == 0, me == peers - 1
    own = rows_scr[me]
    before = jnp.where(first, 0.0, rows_scr[jnp.maximum(me - 1, 0)])
    after = jnp.where(last, 0.0, rows_scr[jnp.minimum(me + 1, peers - 1)])
    lane = iota((8, LANES), 1)
    own = jnp.where(jnp.logical_and(last, lane == LANES - 1), 0.0, own)
    own_left = jnp.where(lane == 0, pltpu.roll(before, 1, 1), pltpu.roll(own, 1, 1))
    after_left = jnp.where(lane == 0, pltpu.roll(own, 1, 1), pltpu.roll(after, 1, 1))
    before_left = pltpu.roll(before, 1, 1)
    ties_ref[0] = own_left + own

    def placed(before, own, after):
        low = jnp.where(lane < HALF + RIM, own, jnp.where(lane >= LANES - RIM, before, 0.0))
        high = jnp.where(lane < RIM, after, jnp.where(lane >= HALF - RIM, own, 0.0))
        return jnp.where(core == 0, low, pltpu.roll(high, HALF, 1))

    ties_ref[1] = placed(before_left, own_left, after_left)
    ties_ref[2] = placed(before, own, after)


def invert_kernel(sky_ref, ties_ref, *refs):
    parts, (out_ref, flat, cells) = refs[:-3], refs[-3:]
    own = out_ref.shape[0]
    knots = math.isqrt(out_ref.shape[1] * LANES)
    total = parts[0][...]
    for part in parts[1:]:
        total = total + part[...]
    flat[...] = jnp.zeros_like(flat)
    flat[0 : own * 8, :] = total.reshape(own * 8, LANES)
    groups = LANES // knots
    for r in range(8):
        turned = flat[pl.ds(r, LANES, stride=8), :].T
        for g in range(groups):
            cells[(8 * g + r) * knots : (8 * g + r + 1) * knots, :] = turned[g * knots : (g + 1) * knots]
    core, chip = lax.rem(sky_ref[0], CORES), sky_ref[0] // CORES
    shift = lax.rem(LANES - core * HALF - chip * own, LANES)
    ties = pltpu.roll(ties_ref[0], shift, 1)
    diagonal = jnp.concatenate([ties] * (knots // 8), axis=0)
    inner = iota((knots, LANES), 0)
    blocks = []
    for k in range(knots):
        row = 0.5 * (cells[k * knots : (k + 1) * knots, :] + cells[pl.ds(k, knots, stride=knots), :])
        blocks.append(jnp.where(inner == k, row + diagonal, row))
    for k in range(knots):
        cells[k * knots : (k + 1) * knots, :] = blocks[k]

    def sweep(k, carry):
        at = pl.multiple_of(k * knots, knots)
        row = cells[pl.ds(at, knots), :]
        pivot = 1.0 / cells[pl.ds(at + k, 1), :]
        here = inner == k
        scaled = jnp.where(here, -pivot, row * pivot)
        for i in range(knots):
            old = jnp.where(here, 0.0, cells[i * knots : (i + 1) * knots, :])
            cells[i * knots : (i + 1) * knots, :] = old - row[i : i + 1] * scaled
        cells[pl.ds(at, knots), :] = scaled
        return carry

    lax.fori_loop(0, knots, sweep, 0)
    for r in range(8):
        turned = jnp.concatenate(
            [cells[(8 * g + r) * knots : (8 * g + r + 1) * knots, :] for g in range(groups)], axis=0
        ).T
        flat[pl.ds(r, LANES, stride=8), :] = -turned
    out_ref[...] = flat[0 : own * 8, :].reshape(own, 8, LANES)


def low_kernel(half, src_ref, out_ref):
    for i in range(src_ref.shape[0]):
        out_ref[:, i * TILE : (i + 1) * TILE] = low_one_hot(src_ref[i : i + 1, :], half, out_ref.shape[0])


def rhs_kernel(hi_count, me_ref, win_ref, low_ref, src_ref, w_ref, r_ref, sp_ref, att_ref, *refs):
    peers = len(refs) - 5
    blocks = refs[:peers]
    out_ref, changes, table, chosen, weighted = refs[peers:]
    half = hi_count * LANES
    windows = LANES
    me = me_ref[0]
    for block, mask in zip(blocks, masks(peers)):
        changes[me ^ mask] = block[...]
    rows = blocks[0].shape[1]
    for j in range(peers):
        q, first = divmod(j * rows, hi_count)
        for p in range(PARAMS):
            value = changes[j, p]
            for s, piece in enumerate(split_bf16(value, SPLITS)):
                start = (s * PARAMS + p) * hi_count + first
                table[start : start + rows, q * LANES : (q + 1) * LANES] = piece.astype(F32)
    lookup = table[...].astype(BF16)

    tiles = src_ref.shape[0]
    window_ids = iota((windows, LANES), 0).astype(F32).astype(BF16)
    chosen[...] = jnp.dot(lookup, low_ref[...], preferred_element_type=F32)
    for i in range(tiles):
        lanes = slice(i * TILE, (i + 1) * TILE)
        columns = sp_ref[:, lanes].astype(F32)
        model = jnp.zeros((hi_count, LANES), F32)
        for p in range(PARAMS):
            value = chosen[p * hi_count : (p + 1) * hi_count, lanes]
            for s in range(1, SPLITS):
                start = (s * PARAMS + p) * hi_count
                value = value + chosen[start : start + hi_count, lanes]
            model = model + value * columns[p : p + 1]
        here = iota((hi_count, LANES), 0) == high_digit(src_ref[i : i + 1, :], half)
        model = jnp.sum(jnp.where(here, model, 0.0), axis=0, keepdims=True)
        change = w_ref[i : i + 1, :] * (r_ref[i : i + 1, :] - model)
        slot = lax.rem(win_ref[i], windows).astype(F32).astype(BF16)
        change = jnp.broadcast_to(change, (windows, LANES)).astype(BF16)
        weighted[:, lanes] = jnp.where(window_ids == slot, change, jnp.zeros((), BF16))
    total = lax.dot_general(att_ref[...], weighted[...], NT, preferred_element_type=F32)
    out_ref[...] = total


def update_kernel(me_ref, sources_ref, *refs):
    blocks, (new_ref, changes) = refs[:-2], refs[-2:]
    for block, mask in zip(blocks, masks(len(blocks))):
        changes[me_ref[0] ^ mask] = block[...]
    rows = blocks[0].shape[1]
    for j in range(len(blocks)):
        for i in range(rows):
            lanes = slice((j * rows + i) * LANES, (j * rows + i + 1) * LANES)
            step = jnp.concatenate([changes[j, p, i : i + 1, :] for p in range(PARAMS)], axis=0)
            new_ref[:, lanes] = sources_ref[:, lanes] + step


def send_kernel(sky_ref, inv_ref, mine_ref, theirs_ref, out_ref):
    own = inv_ref.shape[0]
    core = lax.rem(sky_ref[0], CORES)
    total = mine_ref[...] + theirs_ref[...]
    total = jnp.where(core == 0, total, pltpu.roll(total, HALF, 1))
    packed = narrow(total)
    out_ref[0:own] = inv_ref[...]
    out_ref[own:] = packed.reshape(packed.shape[0] // 8, 8, LANES)


def narrow(x):
    rows = x.shape[0] // 2
    low = iota((rows, LANES), 1) < HALF
    return jnp.where(low, x[:rows], pltpu.roll(x[rows:], HALF, 1))


def widen(x):
    return jnp.concatenate([x, pltpu.roll(x, HALF, 1)], axis=0)


def rim_kernel(sky_ref, *refs):
    chips = len(refs) - 3
    parts, (inner_ref, outer_ref, main_ref) = refs[:chips], refs[chips:]
    own = parts[0].shape[0] - (main_ref.shape[0] - HALF)
    core, chip = lax.rem(sky_ref[0], CORES), sky_ref[0] // CORES
    sides = parts[0][own:]
    for part in parts[1:]:
        sides = sides + part[own:]
    for part, mask in zip(parts, masks(chips)):
        main_ref[pl.ds((chip ^ mask) * own, own)] = part[0:own]
    main_ref[HALF:] = sides
    inner_ref[0:8] = main_ref[pl.ds((1 - core) * (HALF - 8), 8)]
    outer_ref[0:8] = main_ref[pl.ds(core * (HALF - 8), 8)]
    inner_ref[8:] = sides
    outer_ref[8:] = sides


def sweeps_kernel(sky_ref, main_ref, outer_ref, inner_ref, ties_ref, out_ref, flat, cells, vector):
    knots = out_ref.shape[0]
    groups = LANES // knots
    core = lax.rem(sky_ref[0], CORES)
    low = jnp.where(core == 0, outer_ref[...], inner_ref[...])
    high = jnp.where(core == 0, inner_ref[...], outer_ref[...])
    flat[...] = jnp.zeros_like(flat)
    flat[0 : HALF * 8, :] = main_ref[0:HALF].reshape(HALF * 8, LANES)
    flat[HALF * 8 : HALF * 8 + 64, :] = high[0:8].reshape(64, LANES)
    flat[LANES * 8 - 64 : LANES * 8, :] = low[0:8].reshape(64, LANES)
    for r in range(8):
        turned = flat[pl.ds(r, LANES, stride=8), :].T
        for g in range(groups):
            cells[(8 * g + r) * knots : (8 * g + r + 1) * knots, :] = turned[g * knots : (g + 1) * knots]

    def wide(x):
        return widen(x.reshape(knots // 2, LANES))

    lane = iota((knots, LANES), 1)
    sides = jnp.where(lane < HALF, wide(main_ref[HALF:]), 0.0)
    sides = jnp.where(jnp.logical_and(lane >= HALF, lane < HALF + RIM), pltpu.roll(wide(high[8:]), HALF, 1), sides)
    sides = jnp.where(lane >= LANES - RIM, pltpu.roll(wide(low[8:]), HALF, 1), sides)
    left = DAMPING * jnp.concatenate([ties_ref[1]] * (knots // 8), axis=0)
    right = DAMPING * jnp.concatenate([ties_ref[2]] * (knots // 8), axis=0)

    def applied(x):
        vector[...] = x
        total = [jnp.zeros((knots, LANES), F32) for _ in range(4)]
        for k in range(knots):
            total[k % 4] += cells[k * knots : (k + 1) * knots, :] * vector[k : k + 1, :]
        return (total[0] + total[1]) + (total[2] + total[3])

    first = applied(DAMPING * sides)

    def sweep(_, change):
        ends = left * pltpu.roll(change, 1, 1) + right * pltpu.roll(change, LANES - 1, 1)
        return (1.0 - DAMPING) * change + first + applied(ends)

    out_ref[...] = lax.fori_loop(0, ITERS - 1, sweep, first)


def finish_kernel(sky_ref, mine_ref, theirs_ref, attitude_ref, out_ref):
    core = lax.rem(sky_ref[0], CORES)
    lower = jnp.where(core == 0, mine_ref[...], theirs_ref[...])
    upper = jnp.where(core == 0, theirs_ref[...], mine_ref[...])
    lane = iota(lower.shape, 1)
    out_ref[...] = attitude_ref[...] + jnp.where(lane < HALF, lower, pltpu.roll(upper, HALF, 1))


def on_device(
    residuals, weights, source_partials, attitude_partials, source_index, tile_window, sources, attitude, coupling
):
    peers = lax.axis_size("tm")
    devices = lax.axis_size("sky")
    source_count = sources.shape[1]
    windows, knots = attitude.shape
    observations = residuals.shape[0]
    tiles = observations // TILE
    own = windows // devices
    rows = source_count // LANES // peers
    hi_count = source_count // (2 * LANES)
    low_count = 2 * LANES
    me = lax.axis_index("tm").astype(jnp.int32).reshape(1)
    place = lax.axis_index("sky") ^ (lax.axis_index("tm") & 1)
    sky = place.astype(jnp.int32).reshape(1)
    src = source_index.reshape(tiles, TILE)
    w = weights.reshape(tiles, TILE)
    r = residuals.reshape(tiles, TILE)

    chips = devices // CORES
    cell_rows = knots * knots // LANES

    def swapped(blocks):
        return [blocks[0]] + [
            lax.ppermute(block, "tm", [(i, i ^ mask) for i in range(peers)])
            for block, mask in zip(blocks[1:], masks(peers)[1:])
        ]

    def other_core(x):
        return lax.ppermute(x, "sky", [(i, i ^ 1) for i in range(devices)])

    def other_chips(blocks):
        return [blocks[0]] + [
            lax.ppermute(block, "sky", [(i, i ^ (CORES * mask)) for i in range(devices)])
            for block, mask in zip(blocks[1:], masks(chips)[1:])
        ]

    block = jax.ShapeDtypeStruct((MOMENTS + 1, rows, LANES), F32)
    half = jax.ShapeDtypeStruct((HALF, cell_rows, LANES), F32)
    with jax.named_scope("sums"):
        *blocks, keep, give = call(
            functools.partial(sums_kernel, hi_count),
            [block] * peers + [half] * 2,
            [smem()] * 3 + [pl.BlockSpec(memory_space=pl.ANY)] * 6,
            [
                pltpu.VMEM((windows, cell_rows, LANES), F32),
                pltpu.VMEM((SPLITS * MOMENTS * hi_count, observations), BF16),
                pltpu.VMEM((low_count, observations), BF16),
                pltpu.VMEM((SPLITS * MOMENTS * hi_count, low_count), F32),
                pltpu.VMEM((peers, MOMENTS + 1, rows, LANES), F32),
                pltpu.VMEM(src.shape, jnp.int32),
                pltpu.VMEM(w.shape, F32),
                pltpu.VMEM(r.shape, F32),
                pltpu.VMEM(source_partials.shape, BF16),
                pltpu.VMEM(attitude_partials.shape, BF16),
                pltpu.VMEM((1, windows), F32),
                pltpu.SemaphoreType.DMA((6,)),
            ],
            micros=9,
            limit=60 * 1024 * 1024,
        )(me, sky, tile_window, src, w, r, source_partials, attitude_partials, coupling.reshape(1, windows))
    blocks, after_sums = lax.optimization_barrier((blocks, src))
    blocks = swapped(blocks)
    with jax.named_scope("halves"):
        parts = call(
            halves_kernel,
            [jax.ShapeDtypeStruct((own, cell_rows, LANES), F32)] * chips,
            [smem(), vmem(), vmem()],
            [pltpu.VMEM((HALF, cell_rows, LANES), F32)],
        )(sky, keep, other_core(give))
    with jax.named_scope("one_hot"):
        low = call(
            functools.partial(low_kernel, hi_count * LANES),
            jax.ShapeDtypeStruct((low_count, observations), BF16),
            [vmem()],
            micros=1,
        )(after_sums)
    _, low, blocks = lax.optimization_barrier((parts, low, blocks))
    parts = other_chips(parts)
    with jax.named_scope("solve"):
        change, ties = call(
            solve_kernel,
            [
                jax.ShapeDtypeStruct((PARAMS, rows, LANES), F32),
                jax.ShapeDtypeStruct((3, 8, LANES), F32),
            ],
            [smem(), smem()] + [vmem()] * peers,
            [pltpu.VMEM((peers, 8, LANES), F32)],
            micros=30,
        )(me, sky, *blocks)
    changes = swapped([change] * peers)
    with jax.named_scope("invert"):
        inverse = call(
            invert_kernel,
            jax.ShapeDtypeStruct((own, cell_rows, LANES), F32),
            [smem()] + [vmem()] * (1 + chips),
            [pltpu.VMEM((cell_rows * LANES, LANES), F32), pltpu.VMEM((knots * knots, LANES), F32)],
            micros=3,
        )(sky, ties, *parts)
    inverse, changes = lax.optimization_barrier((inverse, changes))
    with jax.named_scope("right_sides"):
        part = call(
            functools.partial(rhs_kernel, hi_count),
            jax.ShapeDtypeStruct((knots, windows), F32),
            [smem(), smem()] + [vmem()] * (6 + peers),
            [
                pltpu.VMEM((peers, PARAMS, rows, LANES), F32),
                pltpu.VMEM((SPLITS * PARAMS * hi_count, low_count), F32),
                pltpu.VMEM((SPLITS * PARAMS * hi_count, observations), F32),
                pltpu.VMEM((windows, observations), BF16),
            ],
            micros=6,
        )(me, tile_window, low, src, w, r, source_partials, attitude_partials, *changes)
    with jax.named_scope("update"):
        changes, part = lax.optimization_barrier((changes, part))
        new_sources = call(
            update_kernel,
            jax.ShapeDtypeStruct(sources.shape, F32),
            [smem()] + [vmem()] * (1 + peers),
            [pltpu.VMEM((peers, PARAMS, rows, LANES), F32)],
        )(me, sources, *changes)
    with jax.named_scope("send"):
        sides = knots // 2 // 8
        sent = call(
            send_kernel,
            jax.ShapeDtypeStruct((own + sides, 8, LANES), F32),
            [smem()] + [vmem()] * 3,
        )(sky, inverse, part, other_core(part))
    got = other_chips([sent] * chips)
    with jax.named_scope("rims"):
        rim = jax.ShapeDtypeStruct((8 + sides, 8, LANES), F32)
        inner, outer, main = call(
            rim_kernel,
            [rim, rim, jax.ShapeDtypeStruct((HALF + sides, 8, LANES), F32)],
            [smem()] + [vmem()] * chips,
        )(sky, *got)
    upper = [(chip * CORES + (1 ^ (t & 1))) * peers + t for chip in range(chips) for t in range(peers - 1)]
    lower = [i + 1 for i in upper]
    outer = lax.ppermute(outer, ("sky", "tm"), list(zip(upper + lower, lower + upper)))
    inner = other_core(inner)
    with jax.named_scope("sweeps"):
        step = call(
            sweeps_kernel,
            jax.ShapeDtypeStruct((knots, LANES), F32),
            [smem()] + [vmem()] * 4,
            [
                pltpu.VMEM((cell_rows * LANES, LANES), F32),
                pltpu.VMEM((knots * knots, LANES), F32),
                pltpu.VMEM((knots, LANES), F32),
            ],
            micros=1,
        )(sky, main, outer, inner, ties)
    with jax.named_scope("finish"):
        new_attitude = call(
            finish_kernel,
            jax.ShapeDtypeStruct((knots, windows), F32),
            [smem()] + [vmem()] * 3,
        )(sky, step, other_core(step), attitude.T)
    return new_sources, new_attitude.T


def solution(mesh):
    return jax.shard_map(
        on_device,
        mesh=mesh,
        in_specs=(
            P(("sky", "tm")),
            P(("sky", "tm")),
            P(None, ("sky", "tm")),
            P(None, ("sky", "tm")),
            P(("sky", "tm")),
            P(("sky", "tm")),
            P(None, "sky"),
            P("tm", None),
            P("tm"),
        ),
        out_specs=(P(None, "sky"), P("tm", None)),
        check_vma=False,
    )
```

```python
import functools
import math

import jax
import jax.numpy as jnp
from jax import lax
from jax.experimental import pallas as pl
from jax.experimental.pallas import tpu as pltpu
from jax.sharding import PartitionSpec as P

TILE = 128
ITERS = 8
RIM = ITERS - 1
DAMPING = 0.8
PARAMS = 5
PAIRS = tuple((i, j) for i in range(PARAMS) for j in range(i + 1))
MOMENTS = len(PAIRS) + PARAMS
LANES = 128
CORES = 2
HALF = LANES // CORES
SPLITS = 2
STEP = 8
ROWS = 8
F32 = jnp.float32
BF16 = jnp.bfloat16
NT = (((1,), (1,)), ((), ()))
FLOPS_MICRO = 1e9
VMEM_LIMIT = 48 * 1024 * 1024


def masks(count):
    return [0] + list(range(count - 1, 0, -1))


def vmem():
    return pl.BlockSpec(memory_space=pltpu.VMEM)


def smem():
    return pl.BlockSpec(memory_space=pltpu.SMEM)


def call(kernel, out_shape, in_specs, scratch=(), micros=0.1, limit=VMEM_LIMIT):
    return pl.pallas_call(
        kernel,
        out_shape=out_shape,
        in_specs=in_specs,
        out_specs=jax.tree.map(lambda _: vmem(), out_shape),
        scratch_shapes=list(scratch),
        compiler_params=pltpu.CompilerParams(vmem_limit_bytes=limit),
        cost_estimate=pl.CostEstimate(flops=int(micros * FLOPS_MICRO), bytes_accessed=0, transcendentals=0),
    )


def iota(shape, dim):
    return lax.broadcasted_iota(jnp.int32, shape, dim)


def split_bf16(x, parts):
    out = []
    for part in range(parts):
        head = x.astype(BF16)
        out.append(head)
        if part < parts - 1:
            x = x - head.astype(F32)
    return out


def low_one_hot(row, half, low_count):
    low = (row // half) * LANES + (row & (LANES - 1))
    return jnp.where(
        iota((low_count, LANES), 0).astype(F32).astype(BF16) == low.astype(F32).astype(BF16),
        jnp.ones((), BF16),
        jnp.zeros((), BF16),
    )


def high_digit(row, half):
    return (row & (half - 1)) // LANES


def sums_kernel(hi_count, me_ref, sky_ref, win_ref, src_hbm, w_hbm, r_hbm, sp_hbm, att_hbm, tie_hbm, *refs):
    peers = len(refs) - 14
    outs, (keep_ref, give_ref, normals, lhs, rhs, acc, blocks) = refs[:peers], refs[peers : peers + 7]
    src_ref, w_ref, r_ref, sp_ref, att_ref, tie_ref, sems = refs[peers + 7 :]
    pairs = (
        (w_hbm, w_ref),
        (att_hbm, att_ref),
        (src_hbm, src_ref),
        (r_hbm, r_ref),
        (sp_hbm, sp_ref),
        (tie_hbm, tie_ref),
    )
    copies = [pltpu.make_async_copy(a, b, sems.at[i]) for i, (a, b) in enumerate(pairs)]
    for copy in copies:
        copy.start()
    normals[...] = jnp.zeros_like(normals)
    for copy in copies[:2]:
        copy.wait()
    window_normals(win_ref, w_ref, att_ref, normals)
    core = lax.rem(sky_ref[0], CORES)
    keep_ref[...] = normals[pl.ds(core * HALF, HALF)]
    give_ref[...] = normals[pl.ds((1 - core) * HALF, HALF)]
    for copy in copies[2:]:
        copy.wait()
    half = hi_count * LANES
    low_count = rhs.shape[0]
    tiles = src_ref.shape[0]
    for base in range(0, tiles, ROWS):
        part = slice(base, base + ROWS)
        src, w, r = src_ref[part, :], w_ref[part, :], r_ref[part, :]
        columns = [sp_ref[:, (base + i) * TILE : (base + i + 1) * TILE].astype(F32) for i in range(ROWS)]
        a = [
            jnp.concatenate([columns[i][p : p + 1] for i in range(ROWS)], axis=0)
            for p in range(PARAMS)
        ]
        wa = [w * x for x in a]
        sums = [wa[i] * a[j] for i, j in PAIRS] + [x * r for x in wa]
        parts = [[piece.astype(F32) for piece in split_bf16(s, SPLITS)] for s in sums]
        for i in range(ROWS):
            lanes = slice((base + i) * TILE, (base + i + 1) * TILE)
            row = src[i : i + 1]
            rhs[:, lanes] = low_one_hot(row, half, low_count)
            mask = jnp.where(iota((hi_count, LANES), 0) == high_digit(row, half), 1.0, 0.0).astype(BF16)
            for s in range(SPLITS):
                for p in range(MOMENTS):
                    value = jnp.broadcast_to(parts[p][s][i : i + 1], (hi_count, LANES)).astype(BF16)
                    start = (s * MOMENTS + p) * hi_count
                    lhs[start : start + hi_count, lanes] = value * mask
    acc[...] = lax.dot_general(lhs[...], rhs[...], NT, preferred_element_type=F32)
    rows = blocks.shape[2]
    for p in range(MOMENTS):
        total = acc[p * hi_count : (p + 1) * hi_count, :]
        for s in range(1, SPLITS):
            start = (s * MOMENTS + p) * hi_count
            total = total + acc[start : start + hi_count, :]
        for j in range(peers):
            q, first = divmod(j * rows, hi_count)
            blocks[j, p] = total[first : first + rows, q * LANES : (q + 1) * LANES]
    for j in range(peers):
        blocks[j, MOMENTS] = jnp.broadcast_to(tie_ref[...], (rows, LANES))
    me = me_ref[0]
    for out, mask in zip(outs, masks(peers)):
        out[...] = blocks[me ^ mask]


def window_normals(win_ref, w_ref, att_ref, sums):
    windows = sums.shape[0]
    knots = att_ref.shape[0]
    copies = LANES // knots
    for t in range(w_ref.shape[0]):
        att = att_ref[:, t * TILE : (t + 1) * TILE]
        scaled = (w_ref[t : t + 1, :] * att.astype(F32)).astype(BF16)
        normal = lax.dot_general(
            jnp.concatenate([scaled, att], axis=1),
            jnp.concatenate([att, scaled], axis=1),
            NT,
            preferred_element_type=F32,
        )
        value = jnp.concatenate([normal[8 * g : 8 * (g + 1)] for g in range(copies)], axis=1)
        sums[lax.rem(win_ref[t], windows)] += value


def halves_kernel(sky_ref, keep_ref, got_ref, *refs):
    outs, total = refs[:-1], refs[-1]
    chip = sky_ref[0] // CORES
    own = outs[0].shape[0]
    total[...] = keep_ref[...] + got_ref[...]
    for out_ref, mask in zip(outs, masks(len(outs))):
        out_ref[...] = total[pl.ds((chip ^ mask) * own, own)]


def solve_kernel(me_ref, sky_ref, *refs):
    peers = len(refs) - 3
    blocks, (change_ref, ties_ref, rows_scr) = refs[:peers], refs[peers:]
    moments = blocks[0][0:MOMENTS]
    for other in blocks[1:]:
        moments = moments + other[0:MOMENTS]
    matrix = {}
    for position, (i, j) in enumerate(PAIRS):
        matrix[i, j] = moments[position] + (1.0 if i == j else 0.0)
    factor, inverse = {}, {}
    for i in range(PARAMS):
        for j in range(i + 1):
            reduced = matrix[i, j]
            for k in range(j):
                reduced = reduced - factor[i, k] * factor[j, k]
            if i == j:
                factor[i, i] = jnp.sqrt(reduced)
                inverse[i] = 1.0 / factor[i, i]
            else:
                factor[i, j] = reduced * inverse[j]
    forward = []
    for i in range(PARAMS):
        current = moments[len(PAIRS) + i]
        for k in range(i):
            current = current - factor[i, k] * forward[k]
        forward.append(current * inverse[i])
    result = [None] * PARAMS
    for i in reversed(range(PARAMS)):
        current = forward[i]
        for k in range(i + 1, PARAMS):
            current = current - factor[k, i] * result[k]
        result[i] = current * inverse[i]
        change_ref[i] = result[i]
    me, core = me_ref[0], lax.rem(sky_ref[0], CORES)
    for block, mask in zip(blocks, masks(peers)):
        rows_scr[me ^ mask] = jnp.broadcast_to(block[MOMENTS, 0:1, :], (8, LANES))
    first, last = me == 0, me == peers - 1
    own = rows_scr[me]
    before = jnp.where(first, 0.0, rows_scr[jnp.maximum(me - 1, 0)])
    after = jnp.where(last, 0.0, rows_scr[jnp.minimum(me + 1, peers - 1)])
    lane = iota((8, LANES), 1)
    own = jnp.where(jnp.logical_and(last, lane == LANES - 1), 0.0, own)
    own_left = jnp.where(lane == 0, pltpu.roll(before, 1, 1), pltpu.roll(own, 1, 1))
    after_left = jnp.where(lane == 0, pltpu.roll(own, 1, 1), pltpu.roll(after, 1, 1))
    before_left = pltpu.roll(before, 1, 1)
    ties_ref[0] = own_left + own

    def placed(before, own, after):
        low = jnp.where(lane < HALF + RIM, own, jnp.where(lane >= LANES - RIM, before, 0.0))
        high = jnp.where(lane < RIM, after, jnp.where(lane >= HALF - RIM, own, 0.0))
        return jnp.where(core == 0, low, pltpu.roll(high, HALF, 1))

    ties_ref[1] = placed(before_left, own_left, after_left)
    ties_ref[2] = placed(before, own, after)


def invert_kernel(sky_ref, ties_ref, *refs):
    parts, (out_ref, flat) = refs[:-2], refs[-2:]
    own = out_ref.shape[0]
    knots = math.isqrt(out_ref.shape[1] * LANES)
    groups = knots // 8
    total = parts[0][...]
    for part in parts[1:]:
        total = total + part[...]
    if own * 8 < LANES:
        flat[...] = jnp.zeros_like(flat)
    flat[0 : own * 8, :] = total.reshape(own * 8, LANES)
    cells = flat[...].T
    core, chip = lax.rem(sky_ref[0], CORES), sky_ref[0] // CORES
    window = core * HALF + chip * own + iota((8, LANES), 1) // 8
    ties = jnp.take_along_axis(ties_ref[0], jnp.minimum(window, LANES - 1), axis=1)
    diagonal = jnp.concatenate([ties] * groups, axis=0)
    column = iota((knots, LANES), 0)
    lane = iota((knots, LANES), 1)
    offset = lane & 7
    rows = [
        0.5 * cells[g * knots : (g + 1) * knots] + jnp.where(column == 8 * g + offset, diagonal, 0.0)
        for g in range(groups)
    ]
    for start in range(0, knots, STEP):
        mine, first = divmod(start, 8)
        pivots = [jnp.take_along_axis(rows[mine], lane - offset + first + i, axis=1) for i in range(STEP)]
        for i in range(STEP):
            k = start + i
            here = column == k
            pivot = 1.0 / pivots[i][k : k + 1]
            scaled = jnp.where(here, -pivot, pivots[i] * pivot)
            rows = [jnp.where(here, 0.0, old) - old[k : k + 1] * scaled for old in rows]
            pivots = [
                scaled if j == i else jnp.where(here, 0.0, old) - old[k : k + 1] * scaled
                for j, old in enumerate(pivots)
            ]
        for i in range(STEP):
            rows[mine] = jnp.where(offset == first + i, pivots[i], rows[mine])
    flat[...] = -jnp.concatenate(rows, axis=0).T
    out_ref[...] = flat[0 : own * 8, :].reshape(own, 8, LANES)


def low_kernel(half, src_ref, out_ref):
    for i in range(src_ref.shape[0]):
        out_ref[:, i * TILE : (i + 1) * TILE] = low_one_hot(src_ref[i : i + 1, :], half, out_ref.shape[0])


def rhs_kernel(hi_count, me_ref, win_ref, low_ref, src_ref, w_ref, r_ref, sp_ref, att_ref, *refs):
    peers = len(refs) - 5
    blocks = refs[:peers]
    out_ref, changes, table, chosen, weighted = refs[peers:]
    half = hi_count * LANES
    windows = LANES
    me = me_ref[0]
    for block, mask in zip(blocks, masks(peers)):
        changes[me ^ mask] = block[...]
    rows = blocks[0].shape[1]
    for j in range(peers):
        q, first = divmod(j * rows, hi_count)
        for p in range(PARAMS):
            value = changes[j, p]
            for s, piece in enumerate(split_bf16(value, SPLITS)):
                start = (s * PARAMS + p) * hi_count + first
                table[start : start + rows, q * LANES : (q + 1) * LANES] = piece.astype(F32)
    lookup = table[...].astype(BF16)

    tiles = src_ref.shape[0]
    window_ids = iota((windows, LANES), 0).astype(F32).astype(BF16)
    chosen[...] = jnp.dot(lookup, low_ref[...], preferred_element_type=F32)
    for i in range(tiles):
        lanes = slice(i * TILE, (i + 1) * TILE)
        columns = sp_ref[:, lanes].astype(F32)
        model = jnp.zeros((hi_count, LANES), F32)
        for p in range(PARAMS):
            value = chosen[p * hi_count : (p + 1) * hi_count, lanes]
            for s in range(1, SPLITS):
                start = (s * PARAMS + p) * hi_count
                value = value + chosen[start : start + hi_count, lanes]
            model = model + value * columns[p : p + 1]
        here = iota((hi_count, LANES), 0) == high_digit(src_ref[i : i + 1, :], half)
        model = jnp.sum(jnp.where(here, model, 0.0), axis=0, keepdims=True)
        change = w_ref[i : i + 1, :] * (r_ref[i : i + 1, :] - model)
        slot = lax.rem(win_ref[i], windows).astype(F32).astype(BF16)
        change = jnp.broadcast_to(change, (windows, LANES)).astype(BF16)
        weighted[:, lanes] = jnp.where(window_ids == slot, change, jnp.zeros((), BF16))
    total = lax.dot_general(att_ref[...], weighted[...], NT, preferred_element_type=F32)
    out_ref[...] = total


def update_kernel(me_ref, sources_ref, *refs):
    blocks, (new_ref, changes) = refs[:-2], refs[-2:]
    for block, mask in zip(blocks, masks(len(blocks))):
        changes[me_ref[0] ^ mask] = block[...]
    rows = blocks[0].shape[1]
    for j in range(len(blocks)):
        for i in range(rows):
            lanes = slice((j * rows + i) * LANES, (j * rows + i + 1) * LANES)
            step = jnp.concatenate([changes[j, p, i : i + 1, :] for p in range(PARAMS)], axis=0)
            new_ref[:, lanes] = sources_ref[:, lanes] + step


def send_kernel(sky_ref, inv_ref, mine_ref, theirs_ref, out_ref):
    own = inv_ref.shape[0]
    core = lax.rem(sky_ref[0], CORES)
    total = mine_ref[...] + theirs_ref[...]
    total = jnp.where(core == 0, total, pltpu.roll(total, HALF, 1))
    packed = narrow(total)
    out_ref[0:own] = inv_ref[...]
    out_ref[own:] = packed.reshape(packed.shape[0] // 8, 8, LANES)


def narrow(x):
    rows = x.shape[0] // 2
    low = iota((rows, LANES), 1) < HALF
    return jnp.where(low, x[:rows], pltpu.roll(x[rows:], HALF, 1))


def widen(x):
    return jnp.concatenate([x, pltpu.roll(x, HALF, 1)], axis=0)


def rim_kernel(sky_ref, *refs):
    chips = len(refs) - 3
    parts, (inner_ref, outer_ref, main_ref) = refs[:chips], refs[chips:]
    own = parts[0].shape[0] - (main_ref.shape[0] - HALF)
    core, chip = lax.rem(sky_ref[0], CORES), sky_ref[0] // CORES
    sides = parts[0][own:]
    for part in parts[1:]:
        sides = sides + part[own:]
    for part, mask in zip(parts, masks(chips)):
        main_ref[pl.ds((chip ^ mask) * own, own)] = part[0:own]
    main_ref[HALF:] = sides
    inner_ref[0:8] = main_ref[pl.ds((1 - core) * (HALF - 8), 8)]
    outer_ref[0:8] = main_ref[pl.ds(core * (HALF - 8), 8)]
    inner_ref[8:] = sides
    outer_ref[8:] = sides


def sweeps_kernel(sky_ref, main_ref, outer_ref, inner_ref, ties_ref, out_ref, flat, cells, vector):
    knots = out_ref.shape[0]
    groups = LANES // knots
    core = lax.rem(sky_ref[0], CORES)
    low = jnp.where(core == 0, outer_ref[...], inner_ref[...])
    high = jnp.where(core == 0, inner_ref[...], outer_ref[...])
    flat[...] = jnp.zeros_like(flat)
    flat[0 : HALF * 8, :] = main_ref[0:HALF].reshape(HALF * 8, LANES)
    flat[HALF * 8 : HALF * 8 + 64, :] = high[0:8].reshape(64, LANES)
    flat[LANES * 8 - 64 : LANES * 8, :] = low[0:8].reshape(64, LANES)
    for r in range(8):
        turned = flat[pl.ds(r, LANES, stride=8), :].T
        for g in range(groups):
            cells[(8 * g + r) * knots : (8 * g + r + 1) * knots, :] = turned[g * knots : (g + 1) * knots]

    def wide(x):
        return widen(x.reshape(knots // 2, LANES))

    lane = iota((knots, LANES), 1)
    sides = jnp.where(lane < HALF, wide(main_ref[HALF:]), 0.0)
    sides = jnp.where(jnp.logical_and(lane >= HALF, lane < HALF + RIM), pltpu.roll(wide(high[8:]), HALF, 1), sides)
    sides = jnp.where(lane >= LANES - RIM, pltpu.roll(wide(low[8:]), HALF, 1), sides)
    left = DAMPING * jnp.concatenate([ties_ref[1]] * (knots // 8), axis=0)
    right = DAMPING * jnp.concatenate([ties_ref[2]] * (knots // 8), axis=0)

    def applied(x):
        vector[...] = x
        total = [jnp.zeros((knots, LANES), F32) for _ in range(4)]
        for k in range(knots):
            total[k % 4] += cells[k * knots : (k + 1) * knots, :] * vector[k : k + 1, :]
        return (total[0] + total[1]) + (total[2] + total[3])

    first = applied(DAMPING * sides)

    def sweep(_, change):
        ends = left * pltpu.roll(change, 1, 1) + right * pltpu.roll(change, LANES - 1, 1)
        return (1.0 - DAMPING) * change + first + applied(ends)

    out_ref[...] = lax.fori_loop(0, ITERS - 1, sweep, first)


def finish_kernel(sky_ref, mine_ref, theirs_ref, attitude_ref, out_ref):
    core = lax.rem(sky_ref[0], CORES)
    lower = jnp.where(core == 0, mine_ref[...], theirs_ref[...])
    upper = jnp.where(core == 0, theirs_ref[...], mine_ref[...])
    lane = iota(lower.shape, 1)
    out_ref[...] = attitude_ref[...] + jnp.where(lane < HALF, lower, pltpu.roll(upper, HALF, 1))


def on_device(
    residuals, weights, source_partials, attitude_partials, source_index, tile_window, sources, attitude, coupling
):
    peers = lax.axis_size("tm")
    devices = lax.axis_size("sky")
    source_count = sources.shape[1]
    windows, knots = attitude.shape
    observations = residuals.shape[0]
    tiles = observations // TILE
    own = windows // devices
    rows = source_count // LANES // peers
    hi_count = source_count // (2 * LANES)
    low_count = 2 * LANES
    me = lax.axis_index("tm").astype(jnp.int32).reshape(1)
    place = lax.axis_index("sky") ^ (lax.axis_index("tm") & 1)
    sky = place.astype(jnp.int32).reshape(1)
    src = source_index.reshape(tiles, TILE)
    w = weights.reshape(tiles, TILE)
    r = residuals.reshape(tiles, TILE)

    chips = devices // CORES
    cell_rows = knots * knots // LANES

    def swapped(blocks):
        return [blocks[0]] + [
            lax.ppermute(block, "tm", [(i, i ^ mask) for i in range(peers)])
            for block, mask in zip(blocks[1:], masks(peers)[1:])
        ]

    def other_core(x):
        return lax.ppermute(x, "sky", [(i, i ^ 1) for i in range(devices)])

    def other_chips(blocks):
        return [blocks[0]] + [
            lax.ppermute(block, "sky", [(i, i ^ (CORES * mask)) for i in range(devices)])
            for block, mask in zip(blocks[1:], masks(chips)[1:])
        ]

    block = jax.ShapeDtypeStruct((MOMENTS + 1, rows, LANES), F32)
    half = jax.ShapeDtypeStruct((HALF, cell_rows, LANES), F32)
    with jax.named_scope("sums"):
        *blocks, keep, give = call(
            functools.partial(sums_kernel, hi_count),
            [block] * peers + [half] * 2,
            [smem()] * 3 + [pl.BlockSpec(memory_space=pl.ANY)] * 6,
            [
                pltpu.VMEM((windows, cell_rows, LANES), F32),
                pltpu.VMEM((SPLITS * MOMENTS * hi_count, observations), BF16),
                pltpu.VMEM((low_count, observations), BF16),
                pltpu.VMEM((SPLITS * MOMENTS * hi_count, low_count), F32),
                pltpu.VMEM((peers, MOMENTS + 1, rows, LANES), F32),
                pltpu.VMEM(src.shape, jnp.int32),
                pltpu.VMEM(w.shape, F32),
                pltpu.VMEM(r.shape, F32),
                pltpu.VMEM(source_partials.shape, BF16),
                pltpu.VMEM(attitude_partials.shape, BF16),
                pltpu.VMEM((1, windows), F32),
                pltpu.SemaphoreType.DMA((6,)),
            ],
            micros=9,
            limit=60 * 1024 * 1024,
        )(me, sky, tile_window, src, w, r, source_partials, attitude_partials, coupling.reshape(1, windows))
    blocks, after_sums = lax.optimization_barrier((blocks, src))
    blocks = swapped(blocks)
    with jax.named_scope("halves"):
        parts = call(
            halves_kernel,
            [jax.ShapeDtypeStruct((own, cell_rows, LANES), F32)] * chips,
            [smem(), vmem(), vmem()],
            [pltpu.VMEM((HALF, cell_rows, LANES), F32)],
        )(sky, keep, other_core(give))
    with jax.named_scope("one_hot"):
        low = call(
            functools.partial(low_kernel, hi_count * LANES),
            jax.ShapeDtypeStruct((low_count, observations), BF16),
            [vmem()],
            micros=1,
        )(after_sums)
    _, low, blocks = lax.optimization_barrier((parts, low, blocks))
    parts = other_chips(parts)
    with jax.named_scope("solve"):
        change, ties = call(
            solve_kernel,
            [
                jax.ShapeDtypeStruct((PARAMS, rows, LANES), F32),
                jax.ShapeDtypeStruct((3, 8, LANES), F32),
            ],
            [smem(), smem()] + [vmem()] * peers,
            [pltpu.VMEM((peers, 8, LANES), F32)],
            micros=30,
        )(me, sky, *blocks)
    changes = swapped([change] * peers)
    with jax.named_scope("invert"):
        inverse = call(
            invert_kernel,
            jax.ShapeDtypeStruct((own, cell_rows, LANES), F32),
            [smem()] + [vmem()] * (1 + chips),
            [pltpu.VMEM((LANES, LANES), F32)],
            micros=3,
        )(sky, ties, *parts)
    inverse, changes = lax.optimization_barrier((inverse, changes))
    with jax.named_scope("right_sides"):
        part = call(
            functools.partial(rhs_kernel, hi_count),
            jax.ShapeDtypeStruct((knots, windows), F32),
            [smem(), smem()] + [vmem()] * (6 + peers),
            [
                pltpu.VMEM((peers, PARAMS, rows, LANES), F32),
                pltpu.VMEM((SPLITS * PARAMS * hi_count, low_count), F32),
                pltpu.VMEM((SPLITS * PARAMS * hi_count, observations), F32),
                pltpu.VMEM((windows, observations), BF16),
            ],
            micros=6,
        )(me, tile_window, low, src, w, r, source_partials, attitude_partials, *changes)
    with jax.named_scope("update"):
        changes, part = lax.optimization_barrier((changes, part))
        new_sources = call(
            update_kernel,
            jax.ShapeDtypeStruct(sources.shape, F32),
            [smem()] + [vmem()] * (1 + peers),
            [pltpu.VMEM((peers, PARAMS, rows, LANES), F32)],
        )(me, sources, *changes)
    with jax.named_scope("send"):
        sides = knots // 2 // 8
        sent = call(
            send_kernel,
            jax.ShapeDtypeStruct((own + sides, 8, LANES), F32),
            [smem()] + [vmem()] * 3,
        )(sky, inverse, part, other_core(part))
    got = other_chips([sent] * chips)
    with jax.named_scope("rims"):
        rim = jax.ShapeDtypeStruct((8 + sides, 8, LANES), F32)
        inner, outer, main = call(
            rim_kernel,
            [rim, rim, jax.ShapeDtypeStruct((HALF + sides, 8, LANES), F32)],
            [smem()] + [vmem()] * chips,
        )(sky, *got)
    upper = [(chip * CORES + (1 ^ (t & 1))) * peers + t for chip in range(chips) for t in range(peers - 1)]
    lower = [i + 1 for i in upper]
    outer = lax.ppermute(outer, ("sky", "tm"), list(zip(upper + lower, lower + upper)))
    inner = other_core(inner)
    with jax.named_scope("sweeps"):
        step = call(
            sweeps_kernel,
            jax.ShapeDtypeStruct((knots, LANES), F32),
            [smem()] + [vmem()] * 4,
            [
                pltpu.VMEM((cell_rows * LANES, LANES), F32),
                pltpu.VMEM((knots * knots, LANES), F32),
                pltpu.VMEM((knots, LANES), F32),
            ],
            micros=1,
        )(sky, main, outer, inner, ties)
    with jax.named_scope("finish"):
        new_attitude = call(
            finish_kernel,
            jax.ShapeDtypeStruct((knots, windows), F32),
            [smem()] + [vmem()] * 3,
        )(sky, step, other_core(step), attitude.T)
    return new_sources, new_attitude.T


def solution(mesh):
    return jax.shard_map(
        on_device,
        mesh=mesh,
        in_specs=(
            P(("sky", "tm")),
            P(("sky", "tm")),
            P(None, ("sky", "tm")),
            P(None, ("sky", "tm")),
            P(("sky", "tm")),
            P(("sky", "tm")),
            P(None, "sky"),
            P("tm", None),
            P("tm"),
        ),
        out_specs=(P(None, "sky"), P("tm", None)),
        check_vma=False,
    )
```

```python
import functools
import math

import jax
import jax.numpy as jnp
from jax import lax
from jax.experimental import pallas as pl
from jax.experimental.pallas import tpu as pltpu
from jax.sharding import PartitionSpec as P

TILE = 128
ITERS = 8
RIM = ITERS - 1
DAMPING = 0.8
PARAMS = 5
PAIRS = tuple((i, j) for i in range(PARAMS) for j in range(i + 1))
MOMENTS = len(PAIRS) + PARAMS
LANES = 128
CORES = 2
HALF = LANES // CORES
SPLITS = 2
STEP = 8
ROWS = 8
F32 = jnp.float32
BF16 = jnp.bfloat16
NT = (((1,), (1,)), ((), ()))
FLOPS_MICRO = 1e9
VMEM_LIMIT = 48 * 1024 * 1024


def masks(count):
    return [0] + list(range(count - 1, 0, -1))


def vmem():
    return pl.BlockSpec(memory_space=pltpu.VMEM)


def smem():
    return pl.BlockSpec(memory_space=pltpu.SMEM)


def call(kernel, out_shape, in_specs, scratch=(), micros=0.1, limit=VMEM_LIMIT):
    return pl.pallas_call(
        kernel,
        out_shape=out_shape,
        in_specs=in_specs,
        out_specs=jax.tree.map(lambda _: vmem(), out_shape),
        scratch_shapes=list(scratch),
        compiler_params=pltpu.CompilerParams(vmem_limit_bytes=limit),
        cost_estimate=pl.CostEstimate(flops=int(micros * FLOPS_MICRO), bytes_accessed=0, transcendentals=0),
    )


def iota(shape, dim):
    return lax.broadcasted_iota(jnp.int32, shape, dim)


def split_bf16(x, parts):
    out = []
    for part in range(parts):
        head = x.astype(BF16)
        out.append(head)
        if part < parts - 1:
            x = x - head.astype(F32)
    return out


def low_one_hot(row, half, low_count):
    low = (row // half) * LANES + (row & (LANES - 1))
    return jnp.where(
        iota((low_count, LANES), 0).astype(F32).astype(BF16) == low.astype(F32).astype(BF16),
        jnp.ones((), BF16),
        jnp.zeros((), BF16),
    )


def high_digit(row, half):
    return (row & (half - 1)) // LANES


def sums_kernel(hi_count, me_ref, sky_ref, win_ref, src_hbm, w_hbm, r_hbm, sp_hbm, att_hbm, tie_hbm, *refs):
    peers = len(refs) - 14
    outs, (keep_ref, give_ref, normals, lhs, rhs, acc, blocks) = refs[:peers], refs[peers : peers + 7]
    src_ref, w_ref, r_ref, sp_ref, att_ref, tie_ref, sems = refs[peers + 7 :]
    pairs = (
        (w_hbm, w_ref),
        (att_hbm, att_ref),
        (src_hbm, src_ref),
        (r_hbm, r_ref),
        (sp_hbm, sp_ref),
        (tie_hbm, tie_ref),
    )
    copies = [pltpu.make_async_copy(a, b, sems.at[i]) for i, (a, b) in enumerate(pairs)]
    for copy in copies:
        copy.start()
    normals[...] = jnp.zeros_like(normals)
    for copy in copies[:2]:
        copy.wait()
    window_normals(win_ref, w_ref, att_ref, normals)
    core = lax.rem(sky_ref[0], CORES)
    keep_ref[...] = normals[pl.ds(core * HALF, HALF)]
    give_ref[...] = normals[pl.ds((1 - core) * HALF, HALF)]
    for copy in copies[2:]:
        copy.wait()
    half = hi_count * LANES
    low_count = rhs.shape[0]
    tiles = src_ref.shape[0]
    for base in range(0, tiles, ROWS):
        part = slice(base, base + ROWS)
        src, w, r = src_ref[part, :], w_ref[part, :], r_ref[part, :]
        columns = [sp_ref[:, (base + i) * TILE : (base + i + 1) * TILE].astype(F32) for i in range(ROWS)]
        a = [
            jnp.concatenate([columns[i][p : p + 1] for i in range(ROWS)], axis=0)
            for p in range(PARAMS)
        ]
        wa = [w * x for x in a]
        sums = [wa[i] * a[j] for i, j in PAIRS] + [x * r for x in wa]
        parts = [[piece.astype(F32) for piece in split_bf16(s, SPLITS)] for s in sums]
        for i in range(ROWS):
            lanes = slice((base + i) * TILE, (base + i + 1) * TILE)
            row = src[i : i + 1]
            rhs[:, lanes] = low_one_hot(row, half, low_count)
            mask = jnp.where(iota((hi_count, LANES), 0) == high_digit(row, half), 1.0, 0.0).astype(BF16)
            for s in range(SPLITS):
                for p in range(MOMENTS):
                    value = jnp.broadcast_to(parts[p][s][i : i + 1], (hi_count, LANES)).astype(BF16)
                    start = (s * MOMENTS + p) * hi_count
                    lhs[start : start + hi_count, lanes] = value * mask
    acc[...] = lax.dot_general(lhs[...], rhs[...], NT, preferred_element_type=F32)
    rows = blocks.shape[2]
    for p in range(MOMENTS):
        total = acc[p * hi_count : (p + 1) * hi_count, :]
        for s in range(1, SPLITS):
            start = (s * MOMENTS + p) * hi_count
            total = total + acc[start : start + hi_count, :]
        for j in range(peers):
            q, first = divmod(j * rows, hi_count)
            blocks[j, p] = total[first : first + rows, q * LANES : (q + 1) * LANES]
    for j in range(peers):
        blocks[j, MOMENTS] = jnp.broadcast_to(tie_ref[...], (rows, LANES))
    me = me_ref[0]
    for out, mask in zip(outs, masks(peers)):
        out[...] = blocks[me ^ mask]


def window_normals(win_ref, w_ref, att_ref, sums):
    windows = sums.shape[0]
    knots = att_ref.shape[0]
    copies = LANES // knots
    for t in range(w_ref.shape[0]):
        att = att_ref[:, t * TILE : (t + 1) * TILE]
        scaled = (w_ref[t : t + 1, :] * att.astype(F32)).astype(BF16)
        normal = lax.dot_general(
            jnp.concatenate([scaled, att], axis=1),
            jnp.concatenate([att, scaled], axis=1),
            NT,
            preferred_element_type=F32,
        )
        value = jnp.concatenate([normal[8 * g : 8 * (g + 1)] for g in range(copies)], axis=1)
        sums[lax.rem(win_ref[t], windows)] += value


def halves_kernel(sky_ref, keep_ref, got_ref, *refs):
    outs, total = refs[:-1], refs[-1]
    chip = sky_ref[0] // CORES
    own = outs[0].shape[0]
    total[...] = keep_ref[...] + got_ref[...]
    for out_ref, mask in zip(outs, masks(len(outs))):
        out_ref[...] = total[pl.ds((chip ^ mask) * own, own)]


def solve_kernel(me_ref, sky_ref, *refs):
    peers = len(refs) - 3
    blocks, (change_ref, ties_ref, rows_scr) = refs[:peers], refs[peers:]
    moments = blocks[0][0:MOMENTS]
    for other in blocks[1:]:
        moments = moments + other[0:MOMENTS]
    matrix = {}
    for position, (i, j) in enumerate(PAIRS):
        matrix[i, j] = moments[position] + (1.0 if i == j else 0.0)
    factor, inverse = {}, {}
    for i in range(PARAMS):
        for j in range(i + 1):
            reduced = matrix[i, j]
            for k in range(j):
                reduced = reduced - factor[i, k] * factor[j, k]
            if i == j:
                factor[i, i] = jnp.sqrt(reduced)
                inverse[i] = 1.0 / factor[i, i]
            else:
                factor[i, j] = reduced * inverse[j]
    forward = []
    for i in range(PARAMS):
        current = moments[len(PAIRS) + i]
        for k in range(i):
            current = current - factor[i, k] * forward[k]
        forward.append(current * inverse[i])
    result = [None] * PARAMS
    for i in reversed(range(PARAMS)):
        current = forward[i]
        for k in range(i + 1, PARAMS):
            current = current - factor[k, i] * result[k]
        result[i] = current * inverse[i]
        change_ref[i] = result[i]
    me, core = me_ref[0], lax.rem(sky_ref[0], CORES)
    for block, mask in zip(blocks, masks(peers)):
        rows_scr[me ^ mask] = jnp.broadcast_to(block[MOMENTS, 0:1, :], (8, LANES))
    first, last = me == 0, me == peers - 1
    own = rows_scr[me]
    before = jnp.where(first, 0.0, rows_scr[jnp.maximum(me - 1, 0)])
    after = jnp.where(last, 0.0, rows_scr[jnp.minimum(me + 1, peers - 1)])
    lane = iota((8, LANES), 1)
    own = jnp.where(jnp.logical_and(last, lane == LANES - 1), 0.0, own)
    own_left = jnp.where(lane == 0, pltpu.roll(before, 1, 1), pltpu.roll(own, 1, 1))
    after_left = jnp.where(lane == 0, pltpu.roll(own, 1, 1), pltpu.roll(after, 1, 1))
    before_left = pltpu.roll(before, 1, 1)
    ties_ref[0] = own_left + own

    def placed(before, own, after):
        low = jnp.where(lane < HALF + RIM, own, jnp.where(lane >= LANES - RIM, before, 0.0))
        high = jnp.where(lane < RIM, after, jnp.where(lane >= HALF - RIM, own, 0.0))
        return jnp.where(core == 0, low, pltpu.roll(high, HALF, 1))

    ties_ref[1] = placed(before_left, own_left, after_left)
    ties_ref[2] = placed(before, own, after)


def lower_blocks(groups):
    return [(g, h) for g in range(groups) for h in range(g + 1)]


def invert_kernel(sky_ref, ties_ref, *refs):
    parts, (out_ref, flat) = refs[:-2], refs[-2:]
    own, cell_rows, _ = parts[0].shape
    knots = math.isqrt(cell_rows * LANES)
    groups = knots // 8
    total = parts[0][...]
    for part in parts[1:]:
        total = total + part[...]
    if own * 8 < LANES:
        flat[...] = jnp.zeros_like(flat)
    flat[0 : own * 8, :] = total.reshape(own * 8, LANES)
    cells = flat[...].T
    core, chip = lax.rem(sky_ref[0], CORES), sky_ref[0] // CORES
    window = core * HALF + chip * own + iota((8, LANES), 1) // 8
    ties = jnp.take_along_axis(ties_ref[0], jnp.minimum(window, LANES - 1), axis=1)
    diagonal = jnp.concatenate([ties] * groups, axis=0)
    column = iota((knots, LANES), 0)
    lane = iota((knots, LANES), 1)
    offset = lane & 7
    rows = [
        0.5 * cells[g * knots : (g + 1) * knots] + jnp.where(column == 8 * g + offset, diagonal, 0.0)
        for g in range(groups)
    ]
    for start in range(0, knots, STEP):
        mine, first = divmod(start, 8)
        pivots = [jnp.take_along_axis(rows[mine], lane - offset + first + i, axis=1) for i in range(STEP)]
        for i in range(STEP):
            k = start + i
            here = column == k
            pivot = 1.0 / pivots[i][k : k + 1]
            scaled = jnp.where(here, -pivot, pivots[i] * pivot)
            rows = [jnp.where(here, 0.0, old) - old[k : k + 1] * scaled for old in rows]
            pivots = [
                scaled if j == i else jnp.where(here, 0.0, old) - old[k : k + 1] * scaled
                for j, old in enumerate(pivots)
            ]
        for i in range(STEP):
            rows[mine] = jnp.where(offset == first + i, pivots[i], rows[mine])
    for at, (g, h) in enumerate(lower_blocks(groups)):
        out_ref[at] = -rows[g][8 * h : 8 * (h + 1)]


def low_kernel(half, src_ref, out_ref):
    for i in range(src_ref.shape[0]):
        out_ref[:, i * TILE : (i + 1) * TILE] = low_one_hot(src_ref[i : i + 1, :], half, out_ref.shape[0])


def rhs_kernel(hi_count, me_ref, win_ref, low_ref, src_ref, w_ref, r_ref, sp_ref, att_ref, *refs):
    peers = len(refs) - 5
    blocks = refs[:peers]
    out_ref, changes, table, chosen, weighted = refs[peers:]
    half = hi_count * LANES
    windows = LANES
    me = me_ref[0]
    for block, mask in zip(blocks, masks(peers)):
        changes[me ^ mask] = block[...]
    rows = blocks[0].shape[1]
    for j in range(peers):
        q, first = divmod(j * rows, hi_count)
        for p in range(PARAMS):
            value = changes[j, p]
            for s, piece in enumerate(split_bf16(value, SPLITS)):
                start = (s * PARAMS + p) * hi_count + first
                table[start : start + rows, q * LANES : (q + 1) * LANES] = piece.astype(F32)
    lookup = table[...].astype(BF16)

    tiles = src_ref.shape[0]
    window_ids = iota((windows, LANES), 0).astype(F32).astype(BF16)
    chosen[...] = jnp.dot(lookup, low_ref[...], preferred_element_type=F32)
    for i in range(tiles):
        lanes = slice(i * TILE, (i + 1) * TILE)
        columns = sp_ref[:, lanes].astype(F32)
        model = jnp.zeros((hi_count, LANES), F32)
        for p in range(PARAMS):
            value = chosen[p * hi_count : (p + 1) * hi_count, lanes]
            for s in range(1, SPLITS):
                start = (s * PARAMS + p) * hi_count
                value = value + chosen[start : start + hi_count, lanes]
            model = model + value * columns[p : p + 1]
        here = iota((hi_count, LANES), 0) == high_digit(src_ref[i : i + 1, :], half)
        model = jnp.sum(jnp.where(here, model, 0.0), axis=0, keepdims=True)
        change = w_ref[i : i + 1, :] * (r_ref[i : i + 1, :] - model)
        slot = lax.rem(win_ref[i], windows).astype(F32).astype(BF16)
        change = jnp.broadcast_to(change, (windows, LANES)).astype(BF16)
        weighted[:, lanes] = jnp.where(window_ids == slot, change, jnp.zeros((), BF16))
    total = lax.dot_general(att_ref[...], weighted[...], NT, preferred_element_type=F32)
    out_ref[...] = total


def update_kernel(me_ref, sources_ref, *refs):
    blocks, (new_ref, changes) = refs[:-2], refs[-2:]
    for block, mask in zip(blocks, masks(len(blocks))):
        changes[me_ref[0] ^ mask] = block[...]
    rows = blocks[0].shape[1]
    for j in range(len(blocks)):
        for i in range(rows):
            lanes = slice((j * rows + i) * LANES, (j * rows + i + 1) * LANES)
            step = jnp.concatenate([changes[j, p, i : i + 1, :] for p in range(PARAMS)], axis=0)
            new_ref[:, lanes] = sources_ref[:, lanes] + step


def send_kernel(sky_ref, inv_ref, mine_ref, theirs_ref, out_ref):
    kept = inv_ref.shape[0]
    core = lax.rem(sky_ref[0], CORES)
    total = mine_ref[...] + theirs_ref[...]
    total = jnp.where(core == 0, total, pltpu.roll(total, HALF, 1))
    packed = narrow(total)
    out_ref[0:kept] = inv_ref[...]
    out_ref[kept:] = packed.reshape(packed.shape[0] // 8, 8, LANES)


def narrow(x):
    rows = x.shape[0] // 2
    low = iota((rows, LANES), 1) < HALF
    return jnp.where(low, x[:rows], pltpu.roll(x[rows:], HALF, 1))


def widen(x):
    return jnp.concatenate([x, pltpu.roll(x, HALF, 1)], axis=0)


def rim_kernel(sky_ref, *refs):
    chips = len(refs) - 3
    parts, (inner_ref, outer_ref, main_ref) = refs[:chips], refs[chips:]
    own = HALF // chips
    kept = parts[0].shape[0] - (main_ref.shape[0] - HALF)
    core, chip = lax.rem(sky_ref[0], CORES), sky_ref[0] // CORES
    sides = parts[0][kept:]
    for part in parts[1:]:
        sides = sides + part[kept:]
    blank = jnp.zeros((LANES - kept * 8, LANES), F32)
    for part, mask in zip(parts, masks(chips)):
        turned = jnp.concatenate([part[0:kept].reshape(kept * 8, LANES), blank], axis=0).T
        main_ref[pl.ds((chip ^ mask) * own, own)] = turned[0 : own * 8].reshape(own, 8, LANES)
    main_ref[HALF:] = sides
    inner_ref[0:8] = main_ref[pl.ds((1 - core) * (HALF - 8), 8)]
    outer_ref[0:8] = main_ref[pl.ds(core * (HALF - 8), 8)]
    inner_ref[8:] = sides
    outer_ref[8:] = sides


def sweeps_kernel(sky_ref, main_ref, outer_ref, inner_ref, ties_ref, out_ref, flat, turns, cells, vector):
    knots = out_ref.shape[0]
    core = lax.rem(sky_ref[0], CORES)
    low = jnp.where(core == 0, outer_ref[...], inner_ref[...])
    high = jnp.where(core == 0, inner_ref[...], outer_ref[...])
    flat[...] = jnp.zeros_like(flat)
    flat[0 : HALF * 8, :] = main_ref[0:HALF].reshape(HALF * 8, LANES)
    flat[HALF * 8 : HALF * 8 + 64, :] = high[0:8].reshape(64, LANES)
    flat[LANES * 8 - 64 : LANES * 8, :] = low[0:8].reshape(64, LANES)
    for r in range(8):
        turns[r * LANES : (r + 1) * LANES, :] = flat[pl.ds(r, LANES, stride=8), :].T
    for at, (g, h) in enumerate(lower_blocks(knots // 8)):
        for r in range(8):
            to = (8 * g + r) * knots + 8 * h
            cells[to : to + 8, :] = turns[r * LANES + 8 * at : r * LANES + 8 * (at + 1), :]
            if g != h:
                to = (8 * h + r) * knots + 8 * g
                cells[to : to + 8, :] = turns[pl.ds(8 * at + r, 8, stride=LANES), :]

    def wide(x):
        return widen(x.reshape(knots // 2, LANES))

    lane = iota((knots, LANES), 1)
    sides = jnp.where(lane < HALF, wide(main_ref[HALF:]), 0.0)
    sides = jnp.where(jnp.logical_and(lane >= HALF, lane < HALF + RIM), pltpu.roll(wide(high[8:]), HALF, 1), sides)
    sides = jnp.where(lane >= LANES - RIM, pltpu.roll(wide(low[8:]), HALF, 1), sides)
    left = DAMPING * jnp.concatenate([ties_ref[1]] * (knots // 8), axis=0)
    right = DAMPING * jnp.concatenate([ties_ref[2]] * (knots // 8), axis=0)

    def applied(x):
        vector[...] = x
        total = [jnp.zeros((knots, LANES), F32) for _ in range(4)]
        for k in range(knots):
            total[k % 4] += cells[k * knots : (k + 1) * knots, :] * vector[k : k + 1, :]
        return (total[0] + total[1]) + (total[2] + total[3])

    first = applied(DAMPING * sides)

    def sweep(_, change):
        ends = left * pltpu.roll(change, 1, 1) + right * pltpu.roll(change, LANES - 1, 1)
        return (1.0 - DAMPING) * change + first + applied(ends)

    out_ref[...] = lax.fori_loop(0, ITERS - 1, sweep, first)


def finish_kernel(sky_ref, mine_ref, theirs_ref, attitude_ref, out_ref):
    core = lax.rem(sky_ref[0], CORES)
    lower = jnp.where(core == 0, mine_ref[...], theirs_ref[...])
    upper = jnp.where(core == 0, theirs_ref[...], mine_ref[...])
    lane = iota(lower.shape, 1)
    out_ref[...] = attitude_ref[...] + jnp.where(lane < HALF, lower, pltpu.roll(upper, HALF, 1))


def on_device(
    residuals, weights, source_partials, attitude_partials, source_index, tile_window, sources, attitude, coupling
):
    peers = lax.axis_size("tm")
    devices = lax.axis_size("sky")
    source_count = sources.shape[1]
    windows, knots = attitude.shape
    observations = residuals.shape[0]
    tiles = observations // TILE
    own = windows // devices
    rows = source_count // LANES // peers
    hi_count = source_count // (2 * LANES)
    low_count = 2 * LANES
    me = lax.axis_index("tm").astype(jnp.int32).reshape(1)
    place = lax.axis_index("sky") ^ (lax.axis_index("tm") & 1)
    sky = place.astype(jnp.int32).reshape(1)
    src = source_index.reshape(tiles, TILE)
    w = weights.reshape(tiles, TILE)
    r = residuals.reshape(tiles, TILE)

    chips = devices // CORES
    cell_rows = knots * knots // LANES

    def swapped(blocks):
        return [blocks[0]] + [
            lax.ppermute(block, "tm", [(i, i ^ mask) for i in range(peers)])
            for block, mask in zip(blocks[1:], masks(peers)[1:])
        ]

    def other_core(x):
        return lax.ppermute(x, "sky", [(i, i ^ 1) for i in range(devices)])

    def other_chips(blocks):
        return [blocks[0]] + [
            lax.ppermute(block, "sky", [(i, i ^ (CORES * mask)) for i in range(devices)])
            for block, mask in zip(blocks[1:], masks(chips)[1:])
        ]

    block = jax.ShapeDtypeStruct((MOMENTS + 1, rows, LANES), F32)
    half = jax.ShapeDtypeStruct((HALF, cell_rows, LANES), F32)
    with jax.named_scope("sums"):
        *blocks, keep, give = call(
            functools.partial(sums_kernel, hi_count),
            [block] * peers + [half] * 2,
            [smem()] * 3 + [pl.BlockSpec(memory_space=pl.ANY)] * 6,
            [
                pltpu.VMEM((windows, cell_rows, LANES), F32),
                pltpu.VMEM((SPLITS * MOMENTS * hi_count, observations), BF16),
                pltpu.VMEM((low_count, observations), BF16),
                pltpu.VMEM((SPLITS * MOMENTS * hi_count, low_count), F32),
                pltpu.VMEM((peers, MOMENTS + 1, rows, LANES), F32),
                pltpu.VMEM(src.shape, jnp.int32),
                pltpu.VMEM(w.shape, F32),
                pltpu.VMEM(r.shape, F32),
                pltpu.VMEM(source_partials.shape, BF16),
                pltpu.VMEM(attitude_partials.shape, BF16),
                pltpu.VMEM((1, windows), F32),
                pltpu.SemaphoreType.DMA((6,)),
            ],
            micros=9,
            limit=60 * 1024 * 1024,
        )(me, sky, tile_window, src, w, r, source_partials, attitude_partials, coupling.reshape(1, windows))
    blocks, after_sums = lax.optimization_barrier((blocks, src))
    blocks = swapped(blocks)
    with jax.named_scope("halves"):
        parts = call(
            halves_kernel,
            [jax.ShapeDtypeStruct((own, cell_rows, LANES), F32)] * chips,
            [smem(), vmem(), vmem()],
            [pltpu.VMEM((HALF, cell_rows, LANES), F32)],
        )(sky, keep, other_core(give))
    with jax.named_scope("one_hot"):
        low = call(
            functools.partial(low_kernel, hi_count * LANES),
            jax.ShapeDtypeStruct((low_count, observations), BF16),
            [vmem()],
            micros=1,
        )(after_sums)
    _, low, blocks = lax.optimization_barrier((parts, low, blocks))
    parts = other_chips(parts)
    with jax.named_scope("solve"):
        change, ties = call(
            solve_kernel,
            [
                jax.ShapeDtypeStruct((PARAMS, rows, LANES), F32),
                jax.ShapeDtypeStruct((3, 8, LANES), F32),
            ],
            [smem(), smem()] + [vmem()] * peers,
            [pltpu.VMEM((peers, 8, LANES), F32)],
            micros=30,
        )(me, sky, *blocks)
    changes = swapped([change] * peers)
    with jax.named_scope("invert"):
        inverse = call(
            invert_kernel,
            jax.ShapeDtypeStruct((len(lower_blocks(knots // 8)), 8, LANES), F32),
            [smem()] + [vmem()] * (1 + chips),
            [pltpu.VMEM((LANES, LANES), F32)],
            micros=3,
        )(sky, ties, *parts)
    inverse, changes = lax.optimization_barrier((inverse, changes))
    with jax.named_scope("right_sides"):
        part = call(
            functools.partial(rhs_kernel, hi_count),
            jax.ShapeDtypeStruct((knots, windows), F32),
            [smem(), smem()] + [vmem()] * (6 + peers),
            [
                pltpu.VMEM((peers, PARAMS, rows, LANES), F32),
                pltpu.VMEM((SPLITS * PARAMS * hi_count, low_count), F32),
                pltpu.VMEM((SPLITS * PARAMS * hi_count, observations), F32),
                pltpu.VMEM((windows, observations), BF16),
            ],
            micros=6,
        )(me, tile_window, low, src, w, r, source_partials, attitude_partials, *changes)
    with jax.named_scope("update"):
        changes, part = lax.optimization_barrier((changes, part))
        new_sources = call(
            update_kernel,
            jax.ShapeDtypeStruct(sources.shape, F32),
            [smem()] + [vmem()] * (1 + peers),
            [pltpu.VMEM((peers, PARAMS, rows, LANES), F32)],
        )(me, sources, *changes)
    with jax.named_scope("send"):
        sides = knots // 2 // 8
        sent = call(
            send_kernel,
            jax.ShapeDtypeStruct((inverse.shape[0] + sides, 8, LANES), F32),
            [smem()] + [vmem()] * 3,
        )(sky, inverse, part, other_core(part))
    got = other_chips([sent] * chips)
    with jax.named_scope("rims"):
        rim = jax.ShapeDtypeStruct((8 + sides, 8, LANES), F32)
        inner, outer, main = call(
            rim_kernel,
            [rim, rim, jax.ShapeDtypeStruct((HALF + sides, 8, LANES), F32)],
            [smem()] + [vmem()] * chips,
        )(sky, *got)
    upper = [(chip * CORES + (1 ^ (t & 1))) * peers + t for chip in range(chips) for t in range(peers - 1)]
    lower = [i + 1 for i in upper]
    outer = lax.ppermute(outer, ("sky", "tm"), list(zip(upper + lower, lower + upper)))
    inner = other_core(inner)
    with jax.named_scope("sweeps"):
        step = call(
            sweeps_kernel,
            jax.ShapeDtypeStruct((knots, LANES), F32),
            [smem()] + [vmem()] * 4,
            [
                pltpu.VMEM((cell_rows * LANES, LANES), F32),
                pltpu.VMEM((cell_rows * LANES, LANES), F32),
                pltpu.VMEM((knots * knots, LANES), F32),
                pltpu.VMEM((knots, LANES), F32),
            ],
            micros=1,
        )(sky, main, outer, inner, ties)
    with jax.named_scope("finish"):
        new_attitude = call(
            finish_kernel,
            jax.ShapeDtypeStruct((knots, windows), F32),
            [smem()] + [vmem()] * 3,
        )(sky, step, other_core(step), attitude.T)
    return new_sources, new_attitude.T


def solution(mesh):
    return jax.shard_map(
        on_device,
        mesh=mesh,
        in_specs=(
            P(("sky", "tm")),
            P(("sky", "tm")),
            P(None, ("sky", "tm")),
            P(None, ("sky", "tm")),
            P(("sky", "tm")),
            P(("sky", "tm")),
            P(None, "sky"),
            P("tm", None),
            P("tm"),
        ),
        out_specs=(P(None, "sky"), P("tm", None)),
        check_vma=False,
    )
```
